32 devices in a mesh: dp: 2 (over core), seq: 16 (over z, y, x).
Axes of the slice: x: 2, y: 2, z: 4, core: 2. Of those that a mesh axis runs over, the one named last changes fastest.
Arguments:
- queries: bfloat16 [16384, 512], P(('dp', 'seq')), parts along dimension 0, may hold values from -12 to 12
- keys: bfloat16 [16384, 512], P(('dp', 'seq')), parts along dimension 0, may hold values from -12 to 12
- values: bfloat16 [16384, 512], P(('dp', 'seq')), parts along dimension 0, may hold values from -6 to 6
- out_grad: bfloat16 [16384, 512], P(('dp', 'seq')), parts along dimension 0, may hold values from -6 to 6
- block_lists: int32 [128, 6], P(('dp', 'seq')), parts along dimension 0, may hold values from -1 to 63, as said below
Outputs:
- attended: bfloat16 [16384, 512], P(('dp', 'seq')), parts along dimension 0
- grad_queries: bfloat16 [16384, 512], P(('dp', 'seq')), parts along dimension 0
- grad_keys: bfloat16 [16384, 512], P(('dp', 'seq')), parts along dimension 0
- grad_values: bfloat16 [16384, 512], P(('dp', 'seq')), parts along dimension 0
The draws below stay inside these ranges and needn't reach their ends.
There are 2 independent parts, one for each index of `dp`. The reference program is written for one: setup_inputs(seed, part) draws one part's arguments, and reference() takes and returns one part's arrays. A program takes and returns all parts, laid end to end along the dimension named above; each array names one. Nothing has to cross between parts.
Inputs may be any that keep to these rules, and one draw needn't show every extreme that they name: `block_lists`: blocks are numbered layer by layer; a calorimeter layer holds 1 to 2 consecutive blocks. Row a lists, in increasing order, every block whose layer is that of block a or next to it, so a itself and only blocks within 3 of a; the relation is symmetric; unused entries come last and are -1; some row uses all 6 entries.
All inputs are finite; a program needn't handle non-finite values.
Results may differ from the reference program's by a relative error of at most 0.02.
Values may be sent and summed in bfloat16 or wider, within the bound.
No kernel may reach another device: no remote copies, remote signals or barrier semaphores. Data moves between devices by JAX's collectives and lax.ppermute only.
A program may use at most 64 MiB of HBM per device.

```python
import jax
import jax.numpy as jnp
from jax import lax

HEADS = 4
HD = 128
BLOCK = 128
LAYER_MOST = 2
KB = 6
REACH = 3
WIDTH = 512
TOKENS = 8192
NBLK = 64


def draw_block_lists(key, part):
    numbers = jnp.arange(NBLK)
    layer_sizes = jax.random.randint(jax.random.fold_in(key, 11), (NBLK,), 1, LAYER_MOST + 1)
    opening = jax.random.randint(jax.random.fold_in(key, 12), (), 0, 3)
    layer_sizes = jnp.where((numbers >= opening) & (numbers < opening + 3), LAYER_MOST, layer_sizes)
    starts = jnp.cumsum(layer_sizes) - layer_sizes
    layer_of = jnp.sum((starts[None, :] <= numbers[:, None]).astype(jnp.int32), axis=1) - 1
    offsets = jnp.arange(-REACH, REACH + 1)
    candidate = numbers[:, None] + offsets[None, :]
    inside = (candidate >= 0) & (candidate < NBLK)
    clipped = jnp.clip(candidate, 0, NBLK - 1)
    related = inside & (jnp.abs(layer_of[clipped] - layer_of[:, None]) <= 1)
    position = jnp.cumsum(related.astype(jnp.int32), axis=1) - 1
    columns = jnp.arange(KB)
    matches = related[:, :, None] & (position[:, :, None] == columns[None, None, :])
    chosen_ids = jnp.sum(jnp.where(matches, candidate[:, :, None] + 1, 0), axis=1) - 1
    return chosen_ids.astype(jnp.int32)


def base_draw(key):
    return jnp.clip(jax.random.normal(key, (TOKENS, HEADS * HD), jnp.float32), -6.0, 6.0)


def draw_queries(key, part):
    result = base_draw(jax.random.fold_in(key, 1))
    return result.astype(jnp.bfloat16)


def draw_keys(key, part):
    result = base_draw(jax.random.fold_in(key, 2))
    return result.astype(jnp.bfloat16)


def steps_of(own_key, dims, cuts, smallest, high):
    factor_of = 1.0
    for dim, shards_of in cuts:
        draws = jax.random.uniform(jax.random.fold_in(jax.random.fold_in(own_key, 6), dim), (shards_of,), jnp.float32, smallest / len(cuts), high / len(cuts))
        factor_of = factor_of * jnp.repeat(jnp.exp(draws), dims[dim] // shards_of).reshape((-1,) + (1,) * (len(dims) - 1 - dim))
    return factor_of


def centred(key, extent, scale, most, shards=(), kind=jnp.bfloat16):
    drawn = jax.random.normal(key, extent, jnp.float32) * scale
    if len(shards) > 0:
        drawn = steps_of(key, extent, shards, -0.22, 0.18) * drawn
    return jnp.clip(drawn, min=-most, max=most).astype(kind)


def setup_inputs(seed: int = 0, part: int = 0) -> dict:
    streams_of = jax.random.split(jax.random.key(seed), 6)
    part_splits = jax.random.split(jax.random.fold_in(streams_of[5], part), 6)
    return {
        "queries": draw_queries(jax.random.fold_in(jax.random.fold_in(streams_of[5], part), 71), part),
        "keys": draw_keys(jax.random.fold_in(jax.random.fold_in(streams_of[5], part), 71), part),
        "values": centred(part_splits[2], (TOKENS, WIDTH), 1.0, 6.0, ((0, 16),)),
        "out_grad": centred(part_splits[3], (TOKENS, WIDTH), 1.0, 6.0, ((0, 16),)),
        "block_lists": draw_block_lists(jax.random.fold_in(jax.random.fold_in(streams_of[5], part), 71), part),
    }


def reference(queries, keys, values, out_grad, block_lists):
    score_scale = HD ** -0.5
    block_count = TOKENS // BLOCK
    width = HEADS * HD
    query_blocks = queries.reshape(block_count, BLOCK, HEADS, HD)
    key_blocks = keys.reshape(block_count, BLOCK, HEADS, HD)
    value_blocks = values.reshape(block_count, BLOCK, HEADS, HD)
    grad_blocks = out_grad.reshape(block_count, BLOCK, HEADS, HD)
    usable = block_lists >= 0
    block_ids = jnp.where(usable, block_lists, 0).astype(jnp.int32)

    def one_block(carry, index):
        key_acc, value_acc = carry
        listed = block_ids[index]
        key_mask = jnp.repeat(usable[index], BLOCK)
        key_rows = key_blocks[listed].reshape(KB * BLOCK, HEADS, HD).astype(jnp.float32)
        value_rows = value_blocks[listed].reshape(KB * BLOCK, HEADS, HD).astype(jnp.float32)
        query_rows = query_blocks[index].astype(jnp.float32)
        grad_rows = grad_blocks[index].astype(jnp.float32)
        scores = jnp.einsum("qhd,khd->hqk", query_rows, key_rows) * score_scale
        scores = jnp.where(key_mask[None, None, :], scores, -jnp.inf)
        peak = jnp.max(scores, axis=-1)
        log_total = peak + jnp.log(jnp.sum(jnp.exp(scores - peak[..., None]), axis=-1))
        probs = jnp.exp(scores - log_total[..., None])
        weights = probs.astype(jnp.bfloat16)
        attended = jnp.einsum("hqk,khd->qhd", weights.astype(jnp.float32), value_rows).astype(jnp.bfloat16)
        row_delta = jnp.sum(grad_rows * attended.astype(jnp.float32), axis=-1)
        grad_probs = jnp.einsum("qhd,khd->hqk", grad_rows, value_rows)
        grad_scores = (probs * (grad_probs - jnp.transpose(row_delta)[:, :, None])).astype(jnp.bfloat16)
        grad_query = (score_scale * jnp.einsum("hqk,khd->qhd", grad_scores.astype(jnp.float32), key_rows)).astype(jnp.bfloat16)
        key_part = score_scale * jnp.einsum("hqk,qhd->khd", grad_scores.astype(jnp.float32), query_rows)
        value_part = jnp.einsum("hqk,qhd->khd", weights.astype(jnp.float32), grad_rows)
        key_acc = key_acc.at[listed].add(key_part.reshape(KB, BLOCK, width))
        value_acc = value_acc.at[listed].add(value_part.reshape(KB, BLOCK, width))
        return (key_acc, value_acc), (attended.reshape(BLOCK, width), grad_query.reshape(BLOCK, width))

    start = (jnp.zeros((block_count, BLOCK, width), jnp.float32), jnp.zeros((block_count, BLOCK, width), jnp.float32))
    (key_acc, value_acc), (attended, grad_queries) = lax.scan(one_block, start, jnp.arange(block_count, dtype=jnp.int32))
    return (attended.reshape(TOKENS, width), grad_queries.reshape(TOKENS, width),
            key_acc.reshape(TOKENS, width).astype(jnp.bfloat16), value_acc.reshape(TOKENS, width).astype(jnp.bfloat16))
```

```python
import functools
import math

import jax
import jax.numpy as jnp
from jax import lax
from jax.experimental import pallas as pl
from jax.experimental.pallas import tpu as pltpu
from jax.sharding import PartitionSpec as P

HEADS = 4
HD = 128
BLOCK = 128
KB = 6
SCALE = HD**-0.5
SCALE2 = SCALE * math.log2(math.e)
NEG = -1e30
F32 = jnp.float32
BF16 = jnp.bfloat16


def dot(a, b, ca, cb):
    return lax.dot_general(a, b, (((ca,), (cb,)), ((), ())), preferred_element_type=F32)


def bias_of(cond):
    return jnp.where(cond, 0.0, NEG).astype(F32)


class Place:
    def __init__(self, lists, nb):
        self.nb = nb
        position = lax.axis_index("seq")
        base = position * nb
        self.has_left = position > 0
        self.has_right = position < lax.axis_size("seq") - 1
        self.lo = [lists[a, 0] - base for a in range(nb)]
        self.hi = []
        for a in range(nb):
            top = lists[a, 0]
            for e in range(1, KB):
                top = jnp.maximum(top, lists[a, e])
            self.hi.append(top - base)
        lo, hi, end = self.lo, self.hi, nb - 1
        self.cut_right = ((lo[end - 1] != lo[end]) | (hi[end - 1] != hi[end])) & (hi[end - 1] >= nb)
        self.cut_left = ((lo[0] != lo[1]) | (hi[0] != hi[1])) & (lo[1] <= -1)
        r, l = self.cut_right.astype(jnp.int32), self.cut_left.astype(jnp.int32)
        self.sent_right = [(0, end - 1 + r), (r, end)]
        self.sent_left = [(1 - l, 0), (1, 1 - l)]
        self.from_left = [(0, -2 + l), (l, -1)]
        self.from_right = [(1 - r, nb), (1, nb + 1 - r)]

    def adjacent(self, own, other):
        return (self.lo[own] <= other) & (other <= self.hi[own])

    def sides(self):
        return (
            (0, 0, self.from_left, 0, self.cut_left),
            (1, self.nb - 3, self.from_right, self.nb - 1, self.cut_right),
        )


def lane(h, half):
    start = (h + 2 * half) * HD
    return pl.ds(start if isinstance(start, int) else pl.multiple_of(start, HD), HD)


def rows_of(b):
    start = b * BLOCK
    return pl.ds(start if isinstance(start, int) else pl.multiple_of(start, BLOCK), BLOCK)


def pack_kernel(nb, lists, q, k, v, g, ra, la, rb, lb):
    at = Place(lists, nb)
    for half, (right, left) in enumerate(((ra, la), (rb, lb))):
        for message, sent in ((right, at.sent_right), (left, at.sent_left)):
            for slot, (h, b) in enumerate(sent):
                for i, array in enumerate((q, k, v, g)):
                    message[2 * i + slot] = array[rows_of(b), lane(h, half)]


def own_forward_kernel(nb, lists, q, k, v, g, stats, ot):
    at = Place(lists, nb)
    biases = [[bias_of(at.adjacent(a, b)) for b in range(nb)] for a in range(nb)]
    for h in range(HEADS):
        cols = lane(h, 0)
        kh, vh = k[:, cols], v[:, cols]
        for a in range(nb):
            rows = rows_of(a)
            s = dot(kh, q[rows, cols], 1, 1)
            s = jnp.concatenate(
                [s[b * BLOCK : (b + 1) * BLOCK] * SCALE2 + biases[a][b] for b in range(nb)], axis=0
            )
            m = jnp.max(s, axis=0, keepdims=True)
            p = jnp.exp2(s - m)
            dp = dot(vh, g[rows, cols], 1, 1)
            stats[h, 0:1, rows] = m
            stats[h, 1:2, rows] = jnp.sum(p, axis=0, keepdims=True)
            stats[h, 2:3, rows] = jnp.sum(p * dp, axis=0, keepdims=True)
            ot[h, :, rows] = dot(vh, p.astype(BF16), 0, 0)


def guest_forward_kernel(
    nb, half, lists, q, k, v, g, in_left, in_right, stats0, ot0, stats, ot, o_left, o_right, st_left, st_right
):
    at = Place(lists, nb)
    for h in range(2):
        stats[h] = stats0[2 * half + h]
        ot[h] = ot0[2 * half + h]
    for side, first, guests, shared, cut in at.sides():
        message = (in_left, in_right)[side]
        o_out = (o_left, o_right)[side]
        st_out = (st_left, st_right)[side]
        span = pl.ds(first * BLOCK, 3 * BLOCK)
        for slot, (h, number) in enumerate(guests):
            qg, kg, vg, gg = (message[2 * i + slot] for i in range(4))
            cols = lane(h, half)
            qh, kh, vh, gh = (array[span, cols] for array in (q, k, v, g))
            near = [at.adjacent(first + b, number) for b in range(3)]
            s = dot(kh, qg, 1, 1)
            s = jnp.concatenate(
                [s[b * BLOCK : (b + 1) * BLOCK] * SCALE2 + bias_of(near[b]) for b in range(3)], axis=0
            )
            m = jnp.max(s, axis=0, keepdims=True)
            p = jnp.exp2(s - m)
            dp = dot(vh, gg, 1, 1)
            total = jnp.sum(p, axis=0, keepdims=True)
            inverse = 1.0 / total
            st_out[2 * slot : 2 * slot + 1, :] = m + jnp.log2(total)
            st_out[2 * slot + 1 : 2 * slot + 2, :] = jnp.sum(p * dp, axis=0, keepdims=True) * inverse
            o_out[slot] = (dot(vh, p.astype(BF16), 0, 0) * inverse).astype(BF16)
            open_ = [
                near[b] & jnp.logical_not(cut) if first + b == shared else near[b] for b in range(3)
            ]
            s = dot(kg, qh, 1, 1)
            s = jnp.concatenate(
                [s[:, b * BLOCK : (b + 1) * BLOCK] * SCALE2 + bias_of(open_[b]) for b in range(3)], axis=1
            )
            old = stats[h, 0:1, span]
            m = jnp.maximum(old, jnp.max(s, axis=0, keepdims=True))
            shrink = jnp.exp2(old - m)
            p = jnp.exp2(s - m)
            dp = dot(vg, gh, 1, 1)
            stats[h, 0:1, span] = m
            stats[h, 1:2, span] = stats[h, 1:2, span] * shrink + jnp.sum(p, axis=0, keepdims=True)
            stats[h, 2:3, span] = stats[h, 2:3, span] * shrink + jnp.sum(p * dp, axis=0, keepdims=True)
            ot[h, :, span] = ot[h, :, span] * shrink + dot(vg, p.astype(BF16), 0, 0)
    for h in range(2):
        total = stats[h, 1:2, :]
        stats[h, 3:4, :] = stats[h, 0:1, :] + jnp.log2(total)
        stats[h, 4:5, :] = stats[h, 2:3, :] / total
    for st_out, sent in ((st_left, at.sent_left), (st_right, at.sent_right)):
        for slot, (h, b) in enumerate(sent):
            rows = rows_of(b)
            st_out[4 + 2 * slot : 5 + 2 * slot, :] = stats[h, 3:4, rows]
            st_out[5 + 2 * slot : 6 + 2 * slot, :] = stats[h, 4:5, rows]


def merged(l1, d1, l2, d2):
    m = jnp.maximum(l1, l2)
    w1, w2 = jnp.exp2(l1 - m), jnp.exp2(l2 - m)
    total = w1 + w2
    return m + jnp.log2(total), (w1 * d1 + w2 * d2) / total


def guest_backward_kernel(
    nb, half, lists, q, k, v, g, in_left, in_right, stats, st_left, st_right, got_left, got_right,
    fin, back_left, back_right, aq, ak, av,
):
    at = Place(lists, nb)
    for array in (aq, ak, av):
        array[...] = jnp.zeros_like(array)
    for h in range(2):
        fin[h, 0:2, :] = stats[h, 3:5, :]
    for got, sent, there in ((got_left, at.sent_left, at.has_left), (got_right, at.sent_right, at.has_right)):
        gone = bias_of(there)
        for slot, (h, b) in enumerate(sent):
            rows = rows_of(b)
            part = got[2 * slot : 2 * slot + 1, :] + gone
            total, delta = merged(
                fin[h, 0:1, rows], fin[h, 1:2, rows], part, got[2 * slot + 1 : 2 * slot + 2, :]
            )
            fin[h, 0:1, rows] = total
            fin[h, 1:2, rows] = delta
    for side, first, guests, shared, cut in at.sides():
        message, back = (in_left, in_right)[side], (back_left, back_right)[side]
        mine, got = (st_left, st_right)[side], (got_left, got_right)[side]
        span = pl.ds(first * BLOCK, 3 * BLOCK)
        for slot, (h, number) in enumerate(guests):
            qg, kg, vg, gg = (message[2 * i + slot] for i in range(4))
            cols = lane(h, half)
            qh, kh, vh, gh = (array[span, cols] for array in (q, k, v, g))
            near = [at.adjacent(first + b, number) for b in range(3)]
            total, delta = merged(
                mine[2 * slot : 2 * slot + 1, :],
                mine[2 * slot + 1 : 2 * slot + 2, :],
                got[4 + 2 * slot : 5 + 2 * slot, :],
                got[5 + 2 * slot : 6 + 2 * slot, :],
            )
            s = dot(kh, qg, 1, 1)
            s = jnp.concatenate(
                [s[b * BLOCK : (b + 1) * BLOCK] * SCALE2 + bias_of(near[b]) for b in range(3)], axis=0
            )
            p = jnp.exp2(s - total)
            ds = (p * (dot(vh, gg, 1, 1) - delta)).astype(BF16)
            ak[h, span, :] += dot(ds, qg, 1, 0)
            av[h, span, :] += dot(p.astype(BF16), gg, 1, 0)
            back[slot] = dot(ds, kh, 0, 0).astype(BF16)
            open_ = [
                near[b] & jnp.logical_not(cut) if first + b == shared else near[b] for b in range(3)
            ]
            s = dot(kg, qh, 1, 1)
            s = jnp.concatenate(
                [s[:, b * BLOCK : (b + 1) * BLOCK] * SCALE2 + bias_of(open_[b]) for b in range(3)], axis=1
            )
            p = jnp.exp2(s - fin[h, 0:1, span])
            ds = (p * (dot(vg, gh, 1, 1) - fin[h, 1:2, span])).astype(BF16)
            back[2 + slot] = dot(ds, qh, 1, 0).astype(BF16)
            back[4 + slot] = dot(p.astype(BF16), gh, 1, 0).astype(BF16)
            aq[h, span, :] += dot(ds, kg, 0, 0)


def own_backward_kernel(
    nb, half, lists, q, k, v, g, stats, ot, fin, o_left, o_right, got_left, got_right, aq0, ak0, av0,
    att, aq, ak, av, total_t, ps, dss,
):
    at = Place(lists, nb)
    biases = [[bias_of(at.adjacent(a, b)) for b in range(nb)] for a in range(nb)]
    for h in range(2):
        total_t[h] = ot[h] * jnp.exp2(stats[h, 0:1, :] - fin[h, 0:1, :])
    for got, o_in, sent, there in (
        (got_left, o_left, at.sent_left, at.has_left),
        (got_right, o_right, at.sent_right, at.has_right),
    ):
        gone = bias_of(there)
        for slot, (h, b) in enumerate(sent):
            rows = rows_of(b)
            weight = jnp.exp2(got[2 * slot : 2 * slot + 1, :] + gone - fin[h, 0:1, rows])
            total_t[h, :, rows] += o_in[slot].astype(F32) * weight
    for h in range(2):
        cols = lane(h, half)
        kh, vh = k[:, cols], v[:, cols]
        for a in range(nb):
            rows = rows_of(a)
            att[rows, lane(h, 0)] = total_t[h, :, rows].T.astype(BF16)
            s = dot(kh, q[rows, cols], 1, 1)
            s = jnp.concatenate(
                [s[b * BLOCK : (b + 1) * BLOCK] * SCALE2 + biases[a][b] for b in range(nb)], axis=0
            )
            p = jnp.exp2(s - fin[h, 0:1, rows])
            ps[:, rows] = p.astype(BF16)
            dss[:, rows] = (p * (dot(vh, g[rows, cols], 1, 1) - fin[h, 1:2, rows])).astype(BF16)
        av[h] = av0[h] + dot(ps[...], g[:, cols], 1, 0)
        ak[h] = ak0[h] + dot(dss[...], q[:, cols], 1, 0)
        aq[h] = aq0[h] + dot(dss[...], kh, 0, 0)


def finish_kernel(nb, lists, *refs):
    at = Place(lists, nb)
    halves = (refs[:6], refs[6:12])
    att_out, q_out, k_out, v_out, sq, sk, sv = refs[12:]
    for half, (att, aq, ak, av, back_left, back_right) in enumerate(halves):
        for h in range(2):
            att_out[:, lane(h, half)] = att[:, lane(h, 0)]
        for total, part in ((sq, aq), (sk, ak), (sv, av)):
            total[...] = part[...]
        for back, sent in ((back_left, at.sent_left), (back_right, at.sent_right)):
            for slot, (h, b) in enumerate(sent):
                rows = rows_of(b)
                for i, total in enumerate((sq, sk, sv)):
                    total[h, rows, :] += back[2 * i + slot].astype(F32)
        for h in range(2):
            cols = lane(h, half)
            q_out[:, cols] = (sq[h] * SCALE).astype(BF16)
            k_out[:, cols] = (sk[h] * SCALE).astype(BF16)
            v_out[:, cols] = sv[h].astype(BF16)


def call(kernel, name, outs, args, scratch=(), flops=0):
    moved = sum(math.prod(s.shape) * s.dtype.itemsize for s in (*outs, *args))
    vmem = pl.BlockSpec(memory_space=pltpu.VMEM)
    return pl.pallas_call(
        kernel,
        out_shape=tuple(outs),
        in_specs=[pl.BlockSpec(memory_space=pltpu.SMEM)] + [vmem] * (len(args) - 1),
        out_specs=tuple([vmem] * len(outs)),
        scratch_shapes=scratch,
        cost_estimate=pl.CostEstimate(flops=flops, bytes_accessed=moved, transcendentals=0),
        compiler_params=pltpu.CompilerParams(vmem_limit_bytes=24 << 20),
        name=name,
    )(*args)


def sds(shape, dtype):
    return jax.ShapeDtypeStruct(shape, dtype)


def body(q, k, v, g, lists):
    rows, width = q.shape
    nb = rows // BLOCK
    count = lax.axis_size("seq")
    forward = [(i, i + 1) for i in range(count - 1)]
    backward = [(i + 1, i) for i in range(count - 1)]

    def swap(to_left, to_right):
        return lax.ppermute(to_right, "seq", forward), lax.ppermute(to_left, "seq", backward)

    arrays = (lists, q, k, v, g)
    tile8 = sds((8, BLOCK, HD), BF16)
    ra, la, rb, lb = call(functools.partial(pack_kernel, nb), "pack", [tile8] * 4, arrays)
    guests = [swap(la, ra), swap(lb, rb)]
    stats0, ot0 = call(
        functools.partial(own_forward_kernel, nb), "own_forward",
        [sds((HEADS, 8, rows), F32), sds((HEADS, HD, rows), F32)], arrays, flops=3 << 30,
    )
    tile2, st = sds((2, BLOCK, HD), BF16), sds((8, HD), F32)
    tile6 = sds((6, BLOCK, HD), BF16)
    acc = sds((2, rows, HD), F32)
    pieces = []
    for half in range(2):
        gl, gr = guests[half]
        stats, ot, o_l, o_r, st_l, st_r = call(
            functools.partial(guest_forward_kernel, nb, half), "guest_forward",
            [sds((2, 8, rows), F32), sds((2, HD, rows), F32), tile2, tile2, st, st],
            (*arrays, gl, gr, stats0, ot0), flops=2 << 30,
        )
        got_l, got_r = swap(st_l, st_r)
        go_l, go_r = swap(o_l, o_r)
        fin, b_l, b_r, aq, ak, av = call(
            functools.partial(guest_backward_kernel, nb, half), "guest_backward",
            [sds((2, 8, rows), F32), tile6, tile6, acc, acc, acc],
            (*arrays, gl, gr, stats, st_l, st_r, got_l, got_r), flops=2 << 30,
        )
        back_l, back_r = swap(b_l, b_r)
        att, aq, ak, av = call(
            functools.partial(own_backward_kernel, nb, half), "own_backward",
            [sds((rows, 2 * HD), BF16), acc, acc, acc],
            (*arrays, stats, ot, fin, go_l, go_r, got_l, got_r, aq, ak, av),
            scratch=(
                pltpu.VMEM((2, HD, rows), F32), pltpu.VMEM((rows, rows), BF16), pltpu.VMEM((rows, rows), BF16),
            ), flops=3 << 30,
        )
        pieces += [att, aq, ak, av, back_l, back_r]
    return call(
        functools.partial(finish_kernel, nb), "finish", [sds((rows, width), BF16)] * 4, (lists, *pieces),
        scratch=tuple(pltpu.VMEM((2, rows, HD), F32) for _ in range(3)),
    )


def solution(mesh):
    spec = P(("dp", "seq"), None)
    return jax.shard_map(
        body, mesh=mesh, in_specs=(spec,) * 5, out_specs=(spec,) * 4, check_vma=False
    )
```

```python
import functools
import math

import jax
import jax.numpy as jnp
from jax import lax
from jax.experimental import pallas as pl
from jax.experimental.pallas import tpu as pltpu
from jax.sharding import PartitionSpec as P

HEADS = 4
HD = 128
BLOCK = 128
KB = 6
SCALE = HD**-0.5
SCALE2 = SCALE * math.log2(math.e)
NEG = -1e30
F32 = jnp.float32
BF16 = jnp.bfloat16


def dot(a, b, ca, cb):
    return lax.dot_general(a, b, (((ca,), (cb,)), ((), ())), preferred_element_type=F32)


def bias_of(cond):
    return jnp.where(cond, 0.0, NEG).astype(F32)


class Place:
    def __init__(self, lists, nb):
        self.nb = nb
        position = lax.axis_index("seq")
        base = position * nb
        self.lo = lo = [lists[a, 0] - base for a in range(nb)]
        self.hi = hi = []
        for a in range(nb):
            top = lists[a, 0]
            for e in range(1, KB):
                top = jnp.maximum(top, lists[a, e])
            hi.append(top - base)
        end = nb - 1
        cut_right = ((lo[end - 1] != lo[end]) | (hi[end - 1] != hi[end])) & (hi[end - 1] >= nb)
        cut_left = ((lo[0] != lo[1]) | (hi[0] != hi[1])) & (lo[1] <= -1)
        r, l = cut_right.astype(jnp.int32), cut_left.astype(jnp.int32)
        odd = lax.rem(position, 2)
        self.partners = []
        for right in (1 - odd, odd):
            is_right = right == 1

            def pick(to_right, to_left):
                return jnp.where(is_right, to_right, to_left)

            partner = Partner()
            partner.there = pick(position < lax.axis_size("seq") - 1, position > 0)
            partner.sent = [(pick(0, 1 - l), pick(end - 1 + r, 0)), (pick(r, 1), pick(end, 1 - l))]
            guests = [(pick(1 - r, 0), pick(nb, -2 + l)), (pick(1, l), pick(nb + 1 - r, -1))]
            first = pick(nb - 3, 0)
            partner.span = pl.ds(pl.multiple_of(first * BLOCK, BLOCK), 3 * BLOCK)
            cut = pick(r, l) == 1
            partner.guests = []
            for h, number in guests:
                near, free = [], []
                for b in range(3):
                    low, high = pick(lo[nb - 3 + b], lo[b]), pick(hi[nb - 3 + b], hi[b])
                    near.append((low <= number) & (number <= high))
                    gone = cut & (is_right if b == 2 else jnp.logical_not(is_right)) if b != 1 else None
                    free.append(near[b] if b == 1 else near[b] & jnp.logical_not(gone))
                partner.guests.append((h, [bias_of(c) for c in near], [bias_of(c) for c in free]))
            self.partners.append(partner)

    def biases(self):
        return [
            [bias_of((self.lo[a] <= b) & (b <= self.hi[a])) for b in range(self.nb)] for a in range(self.nb)
        ]


class Partner:
    pass


def lane(h, half):
    start = (h + 2 * half) * HD
    return pl.ds(start if isinstance(start, int) else pl.multiple_of(start, HD), HD)


def rows_of(b):
    start = b * BLOCK
    return pl.ds(start if isinstance(start, int) else pl.multiple_of(start, BLOCK), BLOCK)


def down(s, biases):
    return jnp.concatenate(
        [s[b * BLOCK : (b + 1) * BLOCK] * SCALE2 + bias for b, bias in enumerate(biases)], axis=0
    )


def across(s, biases):
    return jnp.concatenate(
        [s[:, b * BLOCK : (b + 1) * BLOCK] * SCALE2 + bias for b, bias in enumerate(biases)], axis=1
    )


def total_of(x):
    return jnp.sum(x, axis=0, keepdims=True)


def pack_kernel(nb, half, lists, q, k, v, g, out_a, out_b, sems):
    at = Place(lists, nb)
    copies = []
    for out, partner in zip((out_a, out_b), at.partners):
        for slot, (h, b) in enumerate(partner.sent):
            for i, array in enumerate((q, k, v, g)):
                copy = pltpu.make_async_copy(
                    array.at[rows_of(b), lane(h, half)], out.at[2 * i + slot], sems.at[len(copies)]
                )
                copy.start()
                copies.append(copy)
    for copy in copies:
        copy.wait()


def own_forward_kernel(nb, lists, q, k, v, g, stats, ot):
    at = Place(lists, nb)
    biases = at.biases()
    for h in range(HEADS):
        cols = lane(h, 0)
        kh, vh = k[:, cols], v[:, cols]
        for a in range(nb):
            rows = rows_of(a)
            s = down(dot(kh, q[rows, cols], 1, 1), biases[a])
            m = jnp.max(s, axis=0, keepdims=True)
            p = jnp.exp2(s - m)
            dp = dot(vh, g[rows, cols], 1, 1)
            stats[h, 0:1, rows] = m
            stats[h, 1:2, rows] = total_of(p)
            stats[h, 2:3, rows] = total_of(p * dp)
            ot[h, :, rows] = dot(vh, p.astype(BF16), 0, 0)


def guest_kernel(nb, half, lists, q, k, v, g, in_a, in_b, stats0, ot0, stats, ot, out_a, out_b, st_a, st_b):
    at = Place(lists, nb)
    for h in range(2):
        stats[h] = stats0[2 * half + h]
        ot[h] = ot0[2 * half + h]
    kept = []
    for partner, message, out, st in zip(at.partners, (in_a, in_b), (out_a, out_b), (st_a, st_b)):
        span = partner.span
        for slot, (h, near, free) in enumerate(partner.guests):
            qg, kg, vg, gg = (message[2 * i + slot] for i in range(4))
            cols = lane(h, half)
            qh, kh, vh, gh = (array[span, cols] for array in (q, k, v, g))
            s = down(dot(kh, qg, 1, 1), near)
            m = jnp.max(s, axis=0, keepdims=True)
            p = jnp.exp2(s - m)
            dp = dot(vh, gg, 1, 1)
            total = total_of(p)
            p = p * (1.0 / total)
            delta = total_of(p * dp)
            st[2 * slot : 2 * slot + 1, :] = m + jnp.log2(total)
            st[2 * slot + 1 : 2 * slot + 2, :] = delta
            weights = p.astype(BF16)
            out[slot] = dot(vh, weights, 0, 0).astype(BF16)
            out[2 + slot] = dot(kh, (p * (dp - delta)).astype(BF16), 0, 0).astype(BF16)
            out[4 + slot] = dot(kh, weights, 0, 0).astype(BF16)
            s = across(dot(kg, qh, 1, 1), free)
            old = stats[h, 0:1, span]
            m = jnp.maximum(old, jnp.max(s, axis=0, keepdims=True))
            shrink = jnp.exp2(old - m)
            p = jnp.exp2(s - m)
            dp = dot(vg, gh, 1, 1)
            stats[h, 0:1, span] = m
            stats[h, 1:2, span] = stats[h, 1:2, span] * shrink + total_of(p)
            stats[h, 2:3, span] = stats[h, 2:3, span] * shrink + total_of(p * dp)
            ot[h, :, span] = ot[h, :, span] * shrink + dot(vg, p.astype(BF16), 0, 0)
            kept.append((s, dp, qh, gh))
    for h in range(2):
        total = stats[h, 1:2, :]
        stats[h, 3:4, :] = stats[h, 0:1, :] + jnp.log2(total)
        stats[h, 4:5, :] = stats[h, 2:3, :] / total
    for partner, out, st in zip(at.partners, (out_a, out_b), (st_a, st_b)):
        for slot, (h, near, free) in enumerate(partner.guests):
            s, dp, qh, gh = kept.pop(0)
            p = jnp.exp2(s - stats[h, 3:4, partner.span])
            ds = (p * (dp - stats[h, 4:5, partner.span])).astype(BF16)
            out[6 + slot] = dot(ds, qh, 1, 0).astype(BF16)
            out[8 + slot] = dot(p.astype(BF16), gh, 1, 0).astype(BF16)
        for slot, (h, b) in enumerate(partner.sent):
            st[4 + 2 * slot : 5 + 2 * slot, :] = stats[h, 3:4, rows_of(b)]
            st[5 + 2 * slot : 6 + 2 * slot, :] = stats[h, 4:5, rows_of(b)]


def merged(l1, d1, l2, d2):
    m = jnp.maximum(l1, l2)
    w1, w2 = jnp.exp2(l1 - m), jnp.exp2(l2 - m)
    total = w1 + w2
    return m + jnp.log2(total), (w1 * d1 + w2 * d2) / total


def backward_kernel(
    nb, half, lists, q, k, v, g, in_a, in_b, stats, ot, st_a, st_b, got_a, got_b,
    att, aq, ak, av, mix_a, mix_b, fin, ps, dss,
):
    at = Place(lists, nb)
    biases = at.biases()
    fin[:, 0:2, :] = stats[:, 3:5, :]
    for partner, got, mix in zip(at.partners, (got_a, got_b), (mix_a, mix_b)):
        gone = bias_of(partner.there)
        for slot, (h, b) in enumerate(partner.sent):
            rows = rows_of(b)
            part = got[2 * slot : 2 * slot + 1, :] + gone
            part_delta = got[2 * slot + 1 : 2 * slot + 2, :]
            total, delta = merged(fin[h, 0:1, rows], fin[h, 1:2, rows], part, part_delta)
            fin[h, 0:1, rows] = total
            fin[h, 1:2, rows] = delta
            mix[2 * slot : 2 * slot + 1, :] = jnp.exp2(part - total)
            mix[2 * slot + 1 : 2 * slot + 2, :] = delta - part_delta
    for h in range(2):
        cols = lane(h, half)
        kh, vh = k[:, cols], v[:, cols]
        for a in range(nb):
            rows = rows_of(a)
            own = ot[h, :, rows] * jnp.exp2(stats[h, 0:1, rows] - fin[h, 0:1, rows])
            att[h, rows, :] = own.T
            s = down(dot(kh, q[rows, cols], 1, 1), biases[a])
            p = jnp.exp2(s - fin[h, 0:1, rows])
            ps[:, rows] = p.astype(BF16)
            dss[:, rows] = (p * (dot(vh, g[rows, cols], 1, 1) - fin[h, 1:2, rows])).astype(BF16)
        av[h] = dot(ps[...], g[:, cols], 1, 0)
        ak[h] = dot(dss[...], q[:, cols], 1, 0)
        aq[h] = dot(dss[...], kh, 0, 0)
    for partner, message, mine, got in zip(at.partners, (in_a, in_b), (st_a, st_b), (got_a, got_b)):
        span = partner.span
        for slot, (h, near, free) in enumerate(partner.guests):
            qg, kg, vg, gg = (message[2 * i + slot] for i in range(4))
            cols = lane(h, half)
            qh, kh, vh, gh = (array[span, cols] for array in (q, k, v, g))
            total, delta = merged(
                mine[2 * slot : 2 * slot + 1, :],
                mine[2 * slot + 1 : 2 * slot + 2, :],
                got[4 + 2 * slot : 5 + 2 * slot, :],
                got[5 + 2 * slot : 6 + 2 * slot, :],
            )
            p = jnp.exp2(down(dot(kh, qg, 1, 1), near) - total)
            ds = (p * (dot(vh, gg, 1, 1) - delta)).astype(BF16)
            ak[h, span, :] += dot(ds, qg, 1, 0)
            av[h, span, :] += dot(p.astype(BF16), gg, 1, 0)
            p = jnp.exp2(across(dot(kg, qh, 1, 1), free) - fin[h, 0:1, span])
            ds = (p * (dot(vg, gh, 1, 1) - fin[h, 1:2, span])).astype(BF16)
            aq[h, span, :] += dot(ds, kg, 0, 0)


def finish_kernel(nb, lists, *refs):
    at = Place(lists, nb)
    halves = (refs[:8], refs[8:16])
    att_out, q_out, k_out, v_out, so, sq, sk, sv = refs[16:]
    for half, (att, aq, ak, av, mix_a, mix_b, back_a, back_b) in enumerate(halves):
        for total, part in ((so, att), (sq, aq), (sk, ak), (sv, av)):
            total[...] = part[...]
        for partner, mix, back in zip(at.partners, (mix_a, mix_b), (back_a, back_b)):
            for slot, (h, b) in enumerate(partner.sent):
                rows = rows_of(b)
                o, u, w, dk, dv = (back[2 * i + slot].astype(F32) for i in range(5))
                weight = mix[2 * slot : 2 * slot + 1, :]
                so[h, rows, :] += (o * weight).T
                sq[h, rows, :] += ((u - w * mix[2 * slot + 1 : 2 * slot + 2, :]) * weight).T
                sk[h, rows, :] += dk
                sv[h, rows, :] += dv
        for h in range(2):
            cols = lane(h, half)
            att_out[:, cols] = so[h].astype(BF16)
            q_out[:, cols] = (sq[h] * SCALE).astype(BF16)
            k_out[:, cols] = (sk[h] * SCALE).astype(BF16)
            v_out[:, cols] = sv[h].astype(BF16)


def call(kernel, name, outs, args, scratch=(), flops=0, space=pltpu.VMEM):
    moved = sum(math.prod(s.shape) * s.dtype.itemsize for s in (*outs, *args))
    vmem = pl.BlockSpec(memory_space=pltpu.VMEM)
    return pl.pallas_call(
        kernel,
        out_shape=tuple(outs),
        in_specs=[pl.BlockSpec(memory_space=pltpu.SMEM)]
        + [pl.BlockSpec(memory_space=space)] * (len(args) - 1),
        out_specs=tuple([vmem] * len(outs)),
        scratch_shapes=scratch,
        cost_estimate=pl.CostEstimate(flops=flops, bytes_accessed=moved, transcendentals=0),
        compiler_params=pltpu.CompilerParams(vmem_limit_bytes=24 << 20),
        name=name,
    )(*args)


def sds(shape, dtype):
    return jax.ShapeDtypeStruct(shape, dtype)


def body(q, k, v, g, lists):
    rows, width = q.shape
    nb = rows // BLOCK
    count = lax.axis_size("seq")

    def pairs(start):
        return [(i, j) for a in range(start, count - 1, 2) for i, j in ((a, a + 1), (a + 1, a))]

    def swap(to_a, to_b):
        return lax.ppermute(to_a, "seq", pairs(0)), lax.ppermute(to_b, "seq", pairs(1))

    arrays = (lists, q, k, v, g)
    tile8, tile10 = sds((8, BLOCK, HD), BF16), sds((10, BLOCK, HD), BF16)
    guests = [
        swap(*call(
            functools.partial(pack_kernel, nb, half), "pack", [tile8] * 2, arrays,
            scratch=(pltpu.SemaphoreType.DMA((16,)),), space=pltpu.HBM,
        ))
        for half in range(2)
    ]
    stats0, ot0 = call(
        functools.partial(own_forward_kernel, nb), "own_forward",
        [sds((HEADS, 8, rows), F32), sds((HEADS, HD, rows), F32)], arrays, flops=3 << 30,
    )
    st, acc = sds((8, HD), F32), sds((2, rows, HD), F32)
    forward, backs = [], []
    for half in range(2):
        *kept, out_a, out_b, st_a, st_b = call(
            functools.partial(guest_kernel, nb, half), "guest",
            [sds((2, 8, rows), F32), sds((2, HD, rows), F32), tile10, tile10, st, st],
            (*arrays, *guests[half], stats0, ot0), flops=2 << 30,
        )
        backs.append(swap(out_a, out_b))
        forward.append((*kept, st_a, st_b))
    got = swap(*(jnp.stack([forward[0][i], forward[1][i]]) for i in (2, 3)))
    pieces = []
    for half in range(2):
        outs = call(
            functools.partial(backward_kernel, nb, half), "backward", [acc] * 4 + [st] * 2,
            (*arrays, *guests[half], *forward[half], got[0][half], got[1][half]),
            scratch=(
                pltpu.VMEM((2, 8, rows), F32), pltpu.VMEM((rows, rows), BF16), pltpu.VMEM((rows, rows), BF16),
            ), flops=3 << 30,
        )
        pieces += [*outs, *backs[half]]
    return call(
        functools.partial(finish_kernel, nb), "finish", [sds((rows, width), BF16)] * 4, (lists, *pieces),
        scratch=tuple(pltpu.VMEM((2, rows, HD), F32) for _ in range(4)),
    )


def solution(mesh):
    spec = P(("dp", "seq"), None)
    return jax.shard_map(
        body, mesh=mesh, in_specs=(spec,) * 5, out_specs=(spec,) * 4, check_vma=False
    )
```

```python
import functools
import math

import jax
import jax.numpy as jnp
from jax import lax
from jax.experimental import pallas as pl
from jax.experimental.pallas import tpu as pltpu
from jax.sharding import PartitionSpec as P

HEADS = 4
HD = 128
BLOCK = 128
KB = 6
SCALE = HD**-0.5
SCALE2 = SCALE * math.log2(math.e)
NEG = -1e30
F32 = jnp.float32
BF16 = jnp.bfloat16


def dot(a, b, ca, cb):
    return lax.dot_general(a, b, (((ca,), (cb,)), ((), ())), preferred_element_type=F32)


def bias_of(cond):
    return jnp.where(cond, 0.0, NEG).astype(F32)


class Place:
    def __init__(self, lists, nb):
        self.nb = nb
        position = lax.axis_index("seq")
        base = position * nb
        self.lo = lo = [lists[a, 0] - base for a in range(nb)]
        self.hi = hi = []
        for a in range(nb):
            top = lists[a, 0]
            for e in range(1, KB):
                top = jnp.maximum(top, lists[a, e])
            hi.append(top - base)
        end = nb - 1
        cut_right = ((lo[end - 1] != lo[end]) | (hi[end - 1] != hi[end])) & (hi[end - 1] >= nb)
        cut_left = ((lo[0] != lo[1]) | (hi[0] != hi[1])) & (lo[1] <= -1)
        r, l = cut_right.astype(jnp.int32), cut_left.astype(jnp.int32)
        odd = lax.rem(position, 2)
        self.partners = []
        for right in (1 - odd, odd):
            is_right = right == 1

            def pick(to_right, to_left):
                return jnp.where(is_right, to_right, to_left)

            partner = Partner()
            partner.there = pick(position < lax.axis_size("seq") - 1, position > 0)
            partner.sent = [(pick(0, 1 - l), pick(end - 1 + r, 0)), (pick(r, 1), pick(end, 1 - l))]
            guests = [(pick(1 - r, 0), pick(nb, -2 + l)), (pick(1, l), pick(nb + 1 - r, -1))]
            first = pick(nb - 3, 0)
            partner.span = pl.ds(pl.multiple_of(first * BLOCK, BLOCK), 3 * BLOCK)
            cut = pick(r, l) == 1
            partner.guests = []
            for h, number in guests:
                near, free = [], []
                for b in range(3):
                    low, high = pick(lo[nb - 3 + b], lo[b]), pick(hi[nb - 3 + b], hi[b])
                    near.append((low <= number) & (number <= high))
                    gone = cut & (is_right if b == 2 else jnp.logical_not(is_right)) if b != 1 else None
                    free.append(near[b] if b == 1 else near[b] & jnp.logical_not(gone))
                partner.guests.append((h, [bias_of(c) for c in near], [bias_of(c) for c in free]))
            self.partners.append(partner)

    def biases(self):
        return [
            [bias_of((self.lo[a] <= b) & (b <= self.hi[a])) for b in range(self.nb)] for a in range(self.nb)
        ]


class Partner:
    pass


def lane(h, half):
    start = (h + 2 * half) * HD
    return pl.ds(start if isinstance(start, int) else pl.multiple_of(start, HD), HD)


def rows_of(b):
    start = b * BLOCK
    return pl.ds(start if isinstance(start, int) else pl.multiple_of(start, BLOCK), BLOCK)


def down(s, biases):
    return jnp.concatenate(
        [s[b * BLOCK : (b + 1) * BLOCK] * SCALE2 + bias for b, bias in enumerate(biases)], axis=0
    )


def across(s, biases):
    return jnp.concatenate(
        [s[:, b * BLOCK : (b + 1) * BLOCK] * SCALE2 + bias for b, bias in enumerate(biases)], axis=1
    )


def total_of(x):
    return jnp.sum(x, axis=0, keepdims=True)


def pack_kernel(nb, lists, q, k, v, g, out_a, out_b, sems):
    at = Place(lists, nb)
    copies = []
    for out, partner in zip((out_a, out_b), at.partners):
        for slot, (h, b) in enumerate(partner.sent):
            for i, array in enumerate((q, k, v, g)):
                copy = pltpu.make_async_copy(
                    array.at[rows_of(b), lane(h, 0)], out.at[2 * i + slot], sems.at[len(copies)]
                )
                copy.start()
                copies.append(copy)
    for copy in copies:
        copy.wait()


def own_forward_kernel(nb, lists, q, k, v, g, stats, ot, out_a, out_b):
    at = Place(lists, nb)
    biases = at.biases()
    for out, partner in zip((out_a, out_b), at.partners):
        for slot, (h, b) in enumerate(partner.sent):
            for i, array in enumerate((q, k, v, g)):
                out[2 * i + slot] = array[rows_of(b), lane(h, 1)]
    for h in range(HEADS):
        cols = lane(h, 0)
        kh, vh = k[:, cols], v[:, cols]
        for a in range(nb):
            rows = rows_of(a)
            s = down(dot(kh, q[rows, cols], 1, 1), biases[a])
            m = jnp.max(s, axis=0, keepdims=True)
            p = jnp.exp2(s - m)
            dp = dot(vh, g[rows, cols], 1, 1)
            stats[h, 0:1, rows] = m
            stats[h, 1:2, rows] = total_of(p)
            stats[h, 2:3, rows] = total_of(p * dp)
            ot[h, :, rows] = dot(vh, p.astype(BF16), 0, 0)


def split(x):
    parts = []
    for _ in range(3):
        part = x.astype(BF16)
        parts.append(part)
        x = x - part.astype(F32)
    return parts


TILES = 10 * BLOCK


def guest_kernel(nb, half, lists, q, k, v, g, in_a, in_b, stats0, ot0, stats, ot, out_a, out_b, st_a, st_b):
    at = Place(lists, nb)
    for h in range(2):
        stats[h] = stats0[2 * half + h]
        ot[h] = ot0[2 * half + h]
    kept = []
    for partner, message, out, st in zip(at.partners, (in_a, in_b), (out_a, out_b), (st_a, st_b)):
        span = partner.span
        for slot, (h, near, free) in enumerate(partner.guests):
            qg, kg, vg, gg = (message[2 * i + slot] for i in range(4))
            cols = lane(h, half)
            qh, kh, vh, gh = (array[span, cols] for array in (q, k, v, g))
            s = down(dot(kh, qg, 1, 1), near)
            m = jnp.max(s, axis=0, keepdims=True)
            p = jnp.exp2(s - m)
            dp = dot(vh, gg, 1, 1)
            total = total_of(p)
            p = p * (1.0 / total)
            delta = total_of(p * dp)
            st[2 * slot : 2 * slot + 1, :] = m + jnp.log2(total)
            st[2 * slot + 1 : 2 * slot + 2, :] = delta
            weights = p.astype(BF16)
            out[rows_of(slot), :] = dot(vh, weights, 0, 0).astype(BF16)
            out[rows_of(2 + slot), :] = dot(kh, (p * (dp - delta)).astype(BF16), 0, 0).astype(BF16)
            out[rows_of(4 + slot), :] = dot(kh, weights, 0, 0).astype(BF16)
            s = across(dot(kg, qh, 1, 1), free)
            old = stats[h, 0:1, span]
            m = jnp.maximum(old, jnp.max(s, axis=0, keepdims=True))
            shrink = jnp.exp2(old - m)
            p = jnp.exp2(s - m)
            dp = dot(vg, gh, 1, 1)
            stats[h, 0:1, span] = m
            stats[h, 1:2, span] = stats[h, 1:2, span] * shrink + total_of(p)
            stats[h, 2:3, span] = stats[h, 2:3, span] * shrink + total_of(p * dp)
            ot[h, :, span] = ot[h, :, span] * shrink + dot(vg, p.astype(BF16), 0, 0)
            kept.append((s, dp, qh, gh))
    for h in range(2):
        total = stats[h, 1:2, :]
        stats[h, 3:4, :] = stats[h, 0:1, :] + jnp.log2(total)
        stats[h, 4:5, :] = stats[h, 2:3, :] / total
    for partner, out, st in zip(at.partners, (out_a, out_b), (st_a, st_b)):
        for slot, (h, near, free) in enumerate(partner.guests):
            s, dp, qh, gh = kept.pop(0)
            p = jnp.exp2(s - stats[h, 3:4, partner.span])
            ds = (p * (dp - stats[h, 4:5, partner.span])).astype(BF16)
            out[rows_of(6 + slot), :] = dot(ds, qh, 1, 0).astype(BF16)
            out[rows_of(8 + slot), :] = dot(p.astype(BF16), gh, 1, 0).astype(BF16)
        for slot, (h, b) in enumerate(partner.sent):
            st[4 + 2 * slot : 5 + 2 * slot, :] = stats[h, 3:4, rows_of(b)]
            st[5 + 2 * slot : 6 + 2 * slot, :] = stats[h, 4:5, rows_of(b)]
        if half == 0:
            for i, part in enumerate(split(st[...])):
                out[TILES + 8 * i : TILES + 8 * i + 8, :] = part


def merged(l1, d1, l2, d2):
    m = jnp.maximum(l1, l2)
    w1, w2 = jnp.exp2(l1 - m), jnp.exp2(l2 - m)
    total = w1 + w2
    return m + jnp.log2(total), (w1 * d1 + w2 * d2) / total


def backward_kernel(
    nb, half, lists, q, k, v, g, in_a, in_b, stats, ot, st_a, st_b, came_a, came_b, *refs
):
    att, aq, ak, av, mix_a, mix_b, fin, ps, dss, got_a, got_b = refs[-11:]
    for came, got in ((came_a, got_a), (came_b, got_b)):
        if half == 0:
            parts = [came[TILES + 8 * i : TILES + 8 * i + 8, :].astype(F32) for i in range(3)]
            got[...] = parts[0] + (parts[1] + parts[2])
        else:
            got[...] = came[...]
    at = Place(lists, nb)
    biases = at.biases()
    fin[:, 0:2, :] = stats[:, 3:5, :]
    for partner, got, mix in zip(at.partners, (got_a, got_b), (mix_a, mix_b)):
        gone = bias_of(partner.there)
        for slot, (h, b) in enumerate(partner.sent):
            rows = rows_of(b)
            part = got[2 * slot : 2 * slot + 1, :] + gone
            part_delta = got[2 * slot + 1 : 2 * slot + 2, :]
            total, delta = merged(fin[h, 0:1, rows], fin[h, 1:2, rows], part, part_delta)
            fin[h, 0:1, rows] = total
            fin[h, 1:2, rows] = delta
            mix[2 * slot : 2 * slot + 1, :] = jnp.exp2(part - total)
            mix[2 * slot + 1 : 2 * slot + 2, :] = delta - part_delta
    for h in range(2):
        cols = lane(h, half)
        kh, vh = k[:, cols], v[:, cols]
        for a in range(nb):
            rows = rows_of(a)
            own = ot[h, :, rows] * jnp.exp2(stats[h, 0:1, rows] - fin[h, 0:1, rows])
            att[h, rows, :] = own.T
            s = down(dot(kh, q[rows, cols], 1, 1), biases[a])
            p = jnp.exp2(s - fin[h, 0:1, rows])
            ps[:, rows] = p.astype(BF16)
            dss[:, rows] = (p * (dot(vh, g[rows, cols], 1, 1) - fin[h, 1:2, rows])).astype(BF16)
        av[h] = dot(ps[...], g[:, cols], 1, 0)
        ak[h] = dot(dss[...], q[:, cols], 1, 0)
        aq[h] = dot(dss[...], kh, 0, 0)
    for partner, message, mine, got in zip(at.partners, (in_a, in_b), (st_a, st_b), (got_a, got_b)):
        span = partner.span
        for slot, (h, near, free) in enumerate(partner.guests):
            qg, kg, vg, gg = (message[2 * i + slot] for i in range(4))
            cols = lane(h, half)
            qh, kh, vh, gh = (array[span, cols] for array in (q, k, v, g))
            total, delta = merged(
                mine[2 * slot : 2 * slot + 1, :],
                mine[2 * slot + 1 : 2 * slot + 2, :],
                got[4 + 2 * slot : 5 + 2 * slot, :],
                got[5 + 2 * slot : 6 + 2 * slot, :],
            )
            p = jnp.exp2(down(dot(kh, qg, 1, 1), near) - total)
            ds = (p * (dot(vh, gg, 1, 1) - delta)).astype(BF16)
            ak[h, span, :] += dot(ds, qg, 1, 0)
            av[h, span, :] += dot(p.astype(BF16), gg, 1, 0)
            p = jnp.exp2(across(dot(kg, qh, 1, 1), free) - fin[h, 0:1, span])
            ds = (p * (dot(vg, gh, 1, 1) - fin[h, 1:2, span])).astype(BF16)
            aq[h, span, :] += dot(ds, kg, 0, 0)


def finish_kernel(nb, lists, *refs):
    at = Place(lists, nb)
    halves = (refs[:8], refs[8:16])
    att_out, q_out, k_out, v_out, so, sq, sk, sv = refs[16:]
    for half, (att, aq, ak, av, mix_a, mix_b, back_a, back_b) in enumerate(halves):
        for total, part in ((so, att), (sq, aq), (sk, ak), (sv, av)):
            total[...] = part[...]
        for partner, mix, back in zip(at.partners, (mix_a, mix_b), (back_a, back_b)):
            for slot, (h, b) in enumerate(partner.sent):
                rows = rows_of(b)
                o, u, w, dk, dv = (back[rows_of(2 * i + slot), :].astype(F32) for i in range(5))
                weight = mix[2 * slot : 2 * slot + 1, :]
                so[h, rows, :] += (o * weight).T
                sq[h, rows, :] += ((u - w * mix[2 * slot + 1 : 2 * slot + 2, :]) * weight).T
                sk[h, rows, :] += dk
                sv[h, rows, :] += dv
        for h in range(2):
            cols = lane(h, half)
            att_out[:, cols] = so[h].astype(BF16)
            q_out[:, cols] = (sq[h] * SCALE).astype(BF16)
            k_out[:, cols] = (sk[h] * SCALE).astype(BF16)
            v_out[:, cols] = sv[h].astype(BF16)


def call(kernel, name, outs, args, scratch=(), flops=0, spaces=None, limit=24 << 20, out=pltpu.VMEM):
    moved = sum(math.prod(s.shape) * s.dtype.itemsize for s in (*outs, *args))
    spaces = spaces or (pltpu.SMEM,) + (pltpu.VMEM,) * (len(args) - 1)
    return pl.pallas_call(
        kernel,
        out_shape=tuple(outs),
        in_specs=[pl.BlockSpec(memory_space=space) for space in spaces],
        out_specs=tuple([pl.BlockSpec(memory_space=out)] * len(outs)),
        scratch_shapes=scratch,
        cost_estimate=pl.CostEstimate(flops=flops, bytes_accessed=moved if flops else 1, transcendentals=0),
        compiler_params=pltpu.CompilerParams(vmem_limit_bytes=limit),
        name=name,
    )(*args)


def sds(shape, dtype):
    return jax.ShapeDtypeStruct(shape, dtype)


def body(q, k, v, g, lists):
    rows, width = q.shape
    nb = rows // BLOCK
    count = lax.axis_size("seq")

    def pairs(start):
        return [(i, j) for a in range(start, count - 1, 2) for i, j in ((a, a + 1), (a + 1, a))]

    def swap(to_a, to_b):
        return lax.ppermute(to_a, "seq", pairs(0)), lax.ppermute(to_b, "seq", pairs(1))

    arrays = (lists, q, k, v, g)
    tile8 = sds((8, BLOCK, HD), BF16)
    st, acc = sds((8, HD), F32), sds((2, rows, HD), F32)
    first = call(
        functools.partial(pack_kernel, nb), "pack", [tile8] * 2, arrays,
        scratch=(pltpu.SemaphoreType.DMA((16,)),), spaces=(pltpu.SMEM,) + (pl.ANY,) * 4, limit=60 << 20,
    )
    guests = [swap(*first)]
    stats0, ot0, *second = call(
        functools.partial(own_forward_kernel, nb), "own_forward",
        [sds((HEADS, 8, rows), F32), sds((HEADS, HD, rows), F32), tile8, tile8], arrays, flops=6 << 30,
    )
    guests.append(swap(*second))
    forward, backs = [], []
    for half in range(2):
        result = sds((TILES + 32 * (1 - half), HD), BF16)
        *kept, out_a, out_b, st_a, st_b = call(
            functools.partial(guest_kernel, nb, half), "guest",
            [sds((2, 8, rows), F32), sds((2, HD, rows), F32), result, result, st, st],
            (*arrays, *guests[half], stats0, ot0), flops=4 << 30,
        )
        got = () if half == 0 else swap(st_a, st_b)
        backs.append(swap(out_a, out_b))
        forward.append((*kept, st_a, st_b, *(got or backs[0])))
    pieces, outs = [], ()
    for half in range(2):
        after = outs[-2:]
        outs = call(
            functools.partial(backward_kernel, nb, half), "backward", [acc] * 4 + [st] * 2,
            (*arrays, *guests[half], *forward[half], *after),
            scratch=(
                pltpu.VMEM((2, 8, rows), F32), pltpu.VMEM((rows, rows), BF16), pltpu.VMEM((rows, rows), BF16),
                pltpu.VMEM((8, HD), F32), pltpu.VMEM((8, HD), F32),
            ), flops=(40 << 30, 1 << 30)[half],
            spaces=(pltpu.SMEM,) + (pltpu.VMEM,) * 12 + (pl.ANY,) * len(after),
        )
        pieces += [*outs, *backs[half]]
    return call(
        functools.partial(finish_kernel, nb), "finish", [sds((rows, width), BF16)] * 4, (lists, *pieces),
        scratch=tuple(pltpu.VMEM((2, rows, HD), F32) for _ in range(4)),
    )


def solution(mesh):
    spec = P(("dp", "seq"), None)
    return jax.shard_map(
        body, mesh=mesh, in_specs=(spec,) * 5, out_specs=(spec,) * 4, check_vma=False
    )
```

```python
import functools
import math

import jax
import jax.numpy as jnp
from jax import lax
from jax.experimental import pallas as pl
from jax.experimental.pallas import tpu as pltpu
from jax.sharding import PartitionSpec as P

HEADS = 4
HD = 128
BLOCK = 128
KB = 6
SCALE = HD**-0.5
SCALE2 = SCALE * math.log2(math.e)
NEG = -1e30
F32 = jnp.float32
BF16 = jnp.bfloat16


def dot(a, b, ca, cb):
    return lax.dot_general(a, b, (((ca,), (cb,)), ((), ())), preferred_element_type=F32)


def bias_of(cond):
    return jnp.where(cond, 0.0, NEG).astype(F32)


class Place:
    def __init__(self, lists, nb):
        self.nb = nb
        position = lax.axis_index("seq")
        base = position * nb
        self.lo = lo = [lists[a, 0] - base for a in range(nb)]
        self.hi = hi = []
        for a in range(nb):
            top = lists[a, 0]
            for e in range(1, KB):
                top = jnp.maximum(top, lists[a, e])
            hi.append(top - base)
        end = nb - 1
        cut_right = ((lo[end - 1] != lo[end]) | (hi[end - 1] != hi[end])) & (hi[end - 1] >= nb)
        cut_left = ((lo[0] != lo[1]) | (hi[0] != hi[1])) & (lo[1] <= -1)
        r, l = cut_right.astype(jnp.int32), cut_left.astype(jnp.int32)
        odd = lax.rem(position, 2)
        self.partners = []
        for right in (1 - odd, odd):
            is_right = right == 1

            def pick(to_right, to_left):
                return jnp.where(is_right, to_right, to_left)

            partner = Partner()
            partner.there = pick(position < lax.axis_size("seq") - 1, position > 0)
            partner.sent = [(pick(0, 1 - l), pick(end - 1 + r, 0)), (pick(r, 1), pick(end, 1 - l))]
            guests = [(pick(1 - r, 0), pick(nb, -2 + l)), (pick(1, l), pick(nb + 1 - r, -1))]
            first = pick(nb - 3, 0)
            partner.span = pl.ds(pl.multiple_of(first * BLOCK, BLOCK), 3 * BLOCK)
            cut = pick(r, l) == 1
            partner.guests = []
            for h, number in guests:
                near, free = [], []
                for b in range(3):
                    low, high = pick(lo[nb - 3 + b], lo[b]), pick(hi[nb - 3 + b], hi[b])
                    near.append((low <= number) & (number <= high))
                    gone = cut & (is_right if b == 2 else jnp.logical_not(is_right)) if b != 1 else None
                    free.append(near[b] if b == 1 else near[b] & jnp.logical_not(gone))
                partner.guests.append((h, [bias_of(c) for c in near], [bias_of(c) for c in free]))
            self.partners.append(partner)

    def biases(self):
        return [
            [bias_of((self.lo[a] <= b) & (b <= self.hi[a])) for b in range(self.nb)] for a in range(self.nb)
        ]


class Partner:
    pass


def lane(h, half):
    start = (h + 2 * half) * HD
    return pl.ds(start if isinstance(start, int) else pl.multiple_of(start, HD), HD)


def rows_of(b):
    start = b * BLOCK
    return pl.ds(start if isinstance(start, int) else pl.multiple_of(start, BLOCK), BLOCK)


def down(s, biases):
    return jnp.concatenate(
        [s[b * BLOCK : (b + 1) * BLOCK] * SCALE2 + bias for b, bias in enumerate(biases)], axis=0
    )


def across(s, biases):
    return jnp.concatenate(
        [s[:, b * BLOCK : (b + 1) * BLOCK] * SCALE2 + bias for b, bias in enumerate(biases)], axis=1
    )


def total_of(x):
    return jnp.sum(x, axis=0, keepdims=True)


def pack_kernel(nb, lists, q, k, v, g, out_a, out_b, tiles, sems):
    at = Place(lists, nb)
    copies = []
    for out, partner in zip((out_a, out_b), at.partners):
        for slot, (h, b) in enumerate(partner.sent):
            for i, array in enumerate((q, k, v, g)):
                n = len(copies)
                copy = pltpu.make_async_copy(array.at[rows_of(b), lane(h, 0)], tiles.at[n], sems.at[0, n])
                copy.start()
                copies.append((copy, pltpu.make_async_copy(tiles.at[n], out.at[2 * i + slot], sems.at[1, n])))
    for arrival, departure in copies:
        arrival.wait()
        departure.start()
    for _, departure in copies:
        departure.wait()


def own_forward_kernel(nb, lists, q, k, v, g, stats, ot, out_a, out_b, ps):
    at = Place(lists, nb)
    biases = at.biases()
    for out, partner in zip((out_a, out_b), at.partners):
        for slot, (h, b) in enumerate(partner.sent):
            for i, array in enumerate((q, k, v, g)):
                out[2 * i + slot] = array[rows_of(b), lane(h, 1)]
    for h in range(HEADS):
        cols = lane(h, 0)
        kh, vh = k[:, cols], v[:, cols]
        scores, grads = dot(kh, q[:, cols], 1, 1), dot(vh, g[:, cols], 1, 1)
        for a in range(nb):
            rows = rows_of(a)
            s = down(scores[:, a * BLOCK : (a + 1) * BLOCK], biases[a])
            m = jnp.max(s, axis=0, keepdims=True)
            p = jnp.exp2(s - m)
            stats[h, 0:1, rows] = m
            stats[h, 1:2, rows] = total_of(p)
            stats[h, 2:3, rows] = total_of(p * grads[:, a * BLOCK : (a + 1) * BLOCK])
            ps[:, rows] = p.astype(BF16)
        ot[h] = dot(vh, ps[...], 0, 0)


def split(x):
    parts = []
    for _ in range(3):
        part = x.astype(BF16)
        parts.append(part)
        x = x - part.astype(F32)
    return parts


TILES = 10 * BLOCK


def guest_kernel(nb, half, lists, q, k, v, g, in_a, in_b, stats0, ot0,
                 stats, ot, out_a, out_b, st_a, st_b, aq, pg, dpg):
    at = Place(lists, nb)
    for h in range(2):
        stats[h] = stats0[2 * half + h]
        ot[h] = ot0[2 * half + h]
    aq[...] = jnp.zeros_like(aq)
    kept = []
    for n, (partner, message, out, st) in enumerate(
        zip(at.partners, (in_a, in_b), (out_a, out_b), (st_a, st_b))
    ):
        span = partner.span
        for slot, (h, near, free) in enumerate(partner.guests):
            qg, kg, vg, gg = (message[2 * i + slot] for i in range(4))
            cols = lane(h, half)
            qh, kh, vh, gh = (array[span, cols] for array in (q, k, v, g))
            s = down(dot(kh, qg, 1, 1), near)
            m = jnp.max(s, axis=0, keepdims=True)
            p = jnp.exp2(s - m)
            dp = dot(vh, gg, 1, 1)
            total = total_of(p)
            p = p * (1.0 / total)
            delta = total_of(p * dp)
            st[2 * slot : 2 * slot + 1, :] = m + jnp.log2(total)
            st[2 * slot + 1 : 2 * slot + 2, :] = delta
            weights = p.astype(BF16)
            pg[2 * n + slot] = p
            dpg[2 * n + slot] = dp
            out[rows_of(slot), :] = dot(vh, weights, 0, 0).astype(BF16)
            out[rows_of(2 + slot), :] = dot(kh, (p * (dp - delta)).astype(BF16), 0, 0).astype(BF16)
            out[rows_of(4 + slot), :] = dot(kh, weights, 0, 0).astype(BF16)
            s = across(dot(kg, qh, 1, 1), free)
            old = stats[h, 0:1, span]
            m = jnp.maximum(old, jnp.max(s, axis=0, keepdims=True))
            shrink = jnp.exp2(old - m)
            p = jnp.exp2(s - m)
            dp = dot(vg, gh, 1, 1)
            stats[h, 0:1, span] = m
            stats[h, 1:2, span] = stats[h, 1:2, span] * shrink + total_of(p)
            stats[h, 2:3, span] = stats[h, 2:3, span] * shrink + total_of(p * dp)
            ot[h, :, span] = ot[h, :, span] * shrink + dot(vg, p.astype(BF16), 0, 0)
            kept.append((s, dp, qh, gh, kg))
    for h in range(2):
        total = stats[h, 1:2, :]
        stats[h, 3:4, :] = stats[h, 0:1, :] + jnp.log2(total)
        stats[h, 4:5, :] = stats[h, 2:3, :] / total
    for partner, out, st in zip(at.partners, (out_a, out_b), (st_a, st_b)):
        for slot, (h, near, free) in enumerate(partner.guests):
            s, dp, qh, gh, kg = kept.pop(0)
            p = jnp.exp2(s - stats[h, 3:4, partner.span])
            ds = (p * (dp - stats[h, 4:5, partner.span])).astype(BF16)
            out[rows_of(6 + slot), :] = dot(ds, qh, 1, 0).astype(BF16)
            aq[h, partner.span, :] += dot(ds, kg, 0, 0)
            out[rows_of(8 + slot), :] = dot(p.astype(BF16), gh, 1, 0).astype(BF16)
        for slot, (h, b) in enumerate(partner.sent):
            st[4 + 2 * slot : 5 + 2 * slot, :] = stats[h, 3:4, rows_of(b)]
            st[5 + 2 * slot : 6 + 2 * slot, :] = stats[h, 4:5, rows_of(b)]
        if half == 0:
            for i, part in enumerate(split(st[...])):
                out[TILES + 8 * i : TILES + 8 * i + 8, :] = part


def merged(l1, d1, l2, d2):
    m = jnp.maximum(l1, l2)
    w1, w2 = jnp.exp2(l1 - m), jnp.exp2(l2 - m)
    total = w1 + w2
    return m + jnp.log2(total), (w1 * d1 + w2 * d2) / total


def backward_kernel(
    nb, half, lists, q, k, v, g, in_a, in_b, stats, ot, st_a, st_b, aq0, pg, dpg, came_a, came_b, *refs
):
    att_out, q_out, k_out, v_out, kept, mix_a, mix_b = refs[-16:-9]
    att, aq, ak, av, fin, ps, dss, got_a, got_b = refs[-9:]
    for came, got in ((came_a, got_a), (came_b, got_b)):
        if half == 0:
            parts = [came[TILES + 8 * i : TILES + 8 * i + 8, :].astype(F32) for i in range(3)]
            got[...] = parts[0] + (parts[1] + parts[2])
        else:
            got[...] = came[...]
    at = Place(lists, nb)
    biases = at.biases()
    fin[:, 0:2, :] = stats[:, 3:5, :]
    for partner, got, mix in zip(at.partners, (got_a, got_b), (mix_a, mix_b)):
        gone = bias_of(partner.there)
        for slot, (h, b) in enumerate(partner.sent):
            rows = rows_of(b)
            part = got[2 * slot : 2 * slot + 1, :] + gone
            part_delta = got[2 * slot + 1 : 2 * slot + 2, :]
            total, delta = merged(fin[h, 0:1, rows], fin[h, 1:2, rows], part, part_delta)
            fin[h, 0:1, rows] = total
            fin[h, 1:2, rows] = delta
            mix[2 * slot : 2 * slot + 1, :] = jnp.exp2(part - total)
            mix[2 * slot + 1 : 2 * slot + 2, :] = delta - part_delta
    for h in range(2):
        cols = lane(h, half)
        kh = k[:, cols]
        scores, grads = dot(kh, q[:, cols], 1, 1), dot(v[:, cols], g[:, cols], 1, 1)
        own = ot[h] * jnp.exp2(stats[h, 0:1, :] - fin[h, 0:1, :])
        for a in range(nb):
            rows = rows_of(a)
            here = slice(a * BLOCK, (a + 1) * BLOCK)
            att[h, rows, :] = own[:, here].T
            p = jnp.exp2(down(scores[:, here], biases[a]) - fin[h, 0:1, rows])
            ps[:, rows] = p.astype(BF16)
            dss[:, rows] = (p * (grads[:, here] - fin[h, 1:2, rows])).astype(BF16)
        av[h] = dot(ps[...], g[:, cols], 1, 0)
        ak[h] = dot(dss[...], q[:, cols], 1, 0)
        aq[h] = aq0[h] + dot(dss[...], kh, 0, 0)
    for n, (partner, message, mine, got) in enumerate(
        zip(at.partners, (in_a, in_b), (st_a, st_b), (got_a, got_b))
    ):
        for slot, (h, near, free) in enumerate(partner.guests):
            qg, gg = message[slot], message[6 + slot]
            part = mine[2 * slot : 2 * slot + 1, :]
            total, delta = merged(
                part,
                mine[2 * slot + 1 : 2 * slot + 2, :],
                got[4 + 2 * slot : 5 + 2 * slot, :],
                got[5 + 2 * slot : 6 + 2 * slot, :],
            )
            p = pg[2 * n + slot] * jnp.exp2(part - total)
            ds = (p * (dpg[2 * n + slot] - delta)).astype(BF16)
            ak[h, partner.span, :] += dot(ds, qg, 1, 0)
            av[h, partner.span, :] += dot(p.astype(BF16), gg, 1, 0)
    for h in range(2):
        cols = lane(h, 0)
        att_out[:, cols] = att[h].astype(BF16)
        q_out[:, cols] = (aq[h] * SCALE).astype(BF16)
        k_out[:, cols] = (ak[h] * SCALE).astype(BF16)
        v_out[:, cols] = av[h].astype(BF16)
    for n, partner in enumerate(at.partners):
        for slot, (h, b) in enumerate(partner.sent):
            for i, total in enumerate((att, aq, ak, av)):
                kept[8 * n + 4 * slot + i] = total[h, rows_of(b), :]


def patches(at, kept, mixes, backs):
    for n, (partner, mix, back) in enumerate(zip(at.partners, mixes, backs)):
        for slot, (h, b) in enumerate(partner.sent):
            o, u, w, dk, dv = (back[rows_of(2 * i + slot), :].astype(F32) for i in range(5))
            weight = mix[2 * slot : 2 * slot + 1, :]
            more = mix[2 * slot + 1 : 2 * slot + 2, :]
            whole = ((o * weight).T, ((u - w * more) * weight).T, dk, dv)
            for i, scale in enumerate((1.0, SCALE, SCALE, 1.0)):
                yield h, b, i, ((kept[8 * n + 4 * slot + i] + whole[i]) * scale).astype(BF16)


def finish_first_kernel(nb, lists, *refs):
    at = Place(lists, nb)
    parts, kept, mixes, backs, others, outs = refs[:4], refs[4], refs[5:7], refs[7:9], refs[9:13], refs[13:17]
    for out, part, other in zip(outs, parts, others):
        out[:, : 2 * HD] = part[...]
        out[:, 2 * HD :] = other[...]
    for h, b, i, value in patches(at, kept, mixes, backs):
        outs[i][rows_of(b), lane(h, 0)] = value


def finish_second_kernel(nb, lists, *refs):
    at = Place(lists, nb)
    kept, mixes, backs, outs, tiles, sems = refs[4], refs[5:7], refs[7:9], refs[9:13], refs[13], refs[14]
    copies = []
    for h, b, i, value in patches(at, kept, mixes, backs):
        n = len(copies)
        tiles[n] = value
        copies.append(pltpu.make_async_copy(tiles.at[n], outs[i].at[rows_of(b), lane(h, 1)], sems.at[n]))
        copies[-1].start()
    for copy in copies:
        copy.wait()


def call(kernel, name, outs, args, scratch=(), flops=0, spaces=None, limit=24 << 20, out=pltpu.VMEM, aliases=None):
    moved = sum(math.prod(s.shape) * s.dtype.itemsize for s in (*outs, *args))
    spaces = spaces or (pltpu.SMEM,) + (pltpu.VMEM,) * (len(args) - 1)
    return pl.pallas_call(
        kernel,
        out_shape=tuple(outs),
        in_specs=[pl.BlockSpec(memory_space=space) for space in spaces],
        out_specs=tuple([pl.BlockSpec(memory_space=out)] * len(outs)),
        scratch_shapes=scratch,
        input_output_aliases=aliases or {},
        cost_estimate=pl.CostEstimate(flops=flops, bytes_accessed=moved if flops else 1, transcendentals=0),
        compiler_params=pltpu.CompilerParams(vmem_limit_bytes=limit),
        name=name,
    )(*args)


def sds(shape, dtype):
    return jax.ShapeDtypeStruct(shape, dtype)


def body(q, k, v, g, lists):
    rows, width = q.shape
    nb = rows // BLOCK
    count = lax.axis_size("seq")

    def pairs(start):
        return [(i, j) for a in range(start, count - 1, 2) for i, j in ((a, a + 1), (a + 1, a))]

    def swap(to_a, to_b):
        return lax.ppermute(to_a, "seq", pairs(0)), lax.ppermute(to_b, "seq", pairs(1))

    arrays = (lists, q, k, v, g)
    tile8 = sds((8, BLOCK, HD), BF16)
    st, acc = sds((8, HD), F32), sds((2, rows, HD), F32)
    first = call(
        functools.partial(pack_kernel, nb), "pack", [tile8] * 2, arrays,
        scratch=(pltpu.VMEM((16, BLOCK, HD), BF16), pltpu.SemaphoreType.DMA((2, 16))),
        spaces=(pltpu.SMEM,) + (pl.ANY,) * 4, limit=60 << 20, out=pl.ANY,
    )
    guests = [swap(*first)]
    stats0, ot0, *second = call(
        functools.partial(own_forward_kernel, nb), "own_forward",
        [sds((HEADS, 8, rows), F32), sds((HEADS, HD, rows), F32), tile8, tile8], arrays, flops=6 << 30,
        scratch=(pltpu.VMEM((rows, rows), BF16),),
    )
    guests.append(swap(*second))
    forward, backs = [], []
    for half in range(2):
        result = sds((TILES + 32 * (1 - half), HD), BF16)
        span = (4, 3 * BLOCK, BLOCK)
        *kept, out_a, out_b, st_a, st_b, aq, pg, dpg = call(
            functools.partial(guest_kernel, nb, half), "guest",
            [
                sds((2, 8, rows), F32), sds((2, HD, rows), F32), result, result, st, st,
                acc, sds(span, F32), sds(span, F32),
            ],
            (*arrays, *guests[half], stats0, ot0), flops=4 << 30,
        )
        got = () if half == 0 else swap(st_a, st_b)
        backs.append(swap(out_a, out_b))
        forward.append((*kept, st_a, st_b, aq, pg, dpg, *(got or backs[0])))
    pieces, outs = [], ()
    for half in range(2):
        after = outs[-2:]
        outs = call(
            functools.partial(backward_kernel, nb, half), "backward",
            [sds((rows, 2 * HD), BF16)] * 4 + [sds((16, BLOCK, HD), F32), st, st],
            (*arrays, *guests[half], *forward[half], *after),
            scratch=(
                *(pltpu.VMEM((2, rows, HD), F32) for _ in range(4)), pltpu.VMEM((2, 8, rows), F32),
                pltpu.VMEM((rows, rows), BF16), pltpu.VMEM((rows, rows), BF16),
                pltpu.VMEM((8, HD), F32), pltpu.VMEM((8, HD), F32),
            ), flops=(40 << 30, 1 << 30)[half],
            spaces=(pltpu.SMEM,) + (pltpu.VMEM,) * 15 + (pl.ANY,) * len(after),
        )
        pieces.append((*outs, *backs[half]))
    whole = [sds((rows, width), BF16)] * 4
    outs = call(
        functools.partial(finish_first_kernel, nb), "finish_first", whole, (lists, *pieces[0], *pieces[1][:4])
    )
    return call(
        functools.partial(finish_second_kernel, nb), "finish_second", whole, (lists, *outs, *pieces[1][4:]),
        scratch=(pltpu.VMEM((16, BLOCK, HD), BF16), pltpu.SemaphoreType.DMA((16,))),
        spaces=(pltpu.SMEM,) + (pl.ANY,) * 4 + (pltpu.VMEM,) * 5, out=pl.ANY,
        aliases={i + 1: i for i in range(4)},
    )


def solution(mesh):
    spec = P(("dp", "seq"), None)
    return jax.shard_map(
        body, mesh=mesh, in_specs=(spec,) * 5, out_specs=(spec,) * 4, check_vma=False
    )
```

```python
import functools
import math

import jax
import jax.numpy as jnp
from jax import lax
from jax.experimental import pallas as pl
from jax.experimental.pallas import tpu as pltpu
from jax.sharding import PartitionSpec as P

HEADS = 4
HD = 128
BLOCK = 128
KB = 6
SCALE = HD**-0.5
SCALE2 = SCALE * math.log2(math.e)
NEG = -1e30
F32 = jnp.float32
BF16 = jnp.bfloat16


def dot(a, b, ca, cb):
    return lax.dot_general(a, b, (((ca,), (cb,)), ((), ())), preferred_element_type=F32)


def bias_of(cond):
    return jnp.where(cond, 0.0, NEG).astype(F32)


class Place:
    def __init__(self, lists, nb):
        self.nb = nb
        position = lax.axis_index("seq")
        base = position * nb
        self.lo = lo = [lists[a, 0] - base for a in range(nb)]
        self.hi = hi = []
        for a in range(nb):
            top = lists[a, 0]
            for e in range(1, KB):
                top = jnp.maximum(top, lists[a, e])
            hi.append(top - base)
        end = nb - 1
        cut_right = ((lo[end - 1] != lo[end]) | (hi[end - 1] != hi[end])) & (hi[end - 1] >= nb)
        cut_left = ((lo[0] != lo[1]) | (hi[0] != hi[1])) & (lo[1] <= -1)
        r, l = cut_right.astype(jnp.int32), cut_left.astype(jnp.int32)
        odd = lax.rem(position, 2)
        self.partners = []
        for right in (1 - odd, odd):
            is_right = right == 1

            def pick(to_right, to_left):
                return jnp.where(is_right, to_right, to_left)

            partner = Partner()
            partner.there = pick(position < lax.axis_size("seq") - 1, position > 0)
            partner.sent = [(pick(0, 1 - l), pick(end - 1 + r, 0)), (pick(r, 1), pick(end, 1 - l))]
            guests = [(pick(1 - r, 0), pick(nb, -2 + l)), (pick(1, l), pick(nb + 1 - r, -1))]
            first = pick(nb - 3, 0)
            partner.span = pl.ds(pl.multiple_of(first * BLOCK, BLOCK), 3 * BLOCK)
            cut = pick(r, l) == 1
            partner.guests = []
            for h, number in guests:
                near, free = [], []
                for b in range(3):
                    low, high = pick(lo[nb - 3 + b], lo[b]), pick(hi[nb - 3 + b], hi[b])
                    near.append((low <= number) & (number <= high))
                    gone = cut & (is_right if b == 2 else jnp.logical_not(is_right)) if b != 1 else None
                    free.append(near[b] if b == 1 else near[b] & jnp.logical_not(gone))
                partner.guests.append((h, [bias_of(c) for c in near], [bias_of(c) for c in free]))
            self.partners.append(partner)

    def biases(self):
        return [
            [bias_of((self.lo[a] <= b) & (b <= self.hi[a])) for b in range(self.nb)] for a in range(self.nb)
        ]


class Partner:
    pass


def lane(h, half):
    start = (h + 2 * half) * HD
    return pl.ds(start if isinstance(start, int) else pl.multiple_of(start, HD), HD)


def rows_of(b):
    start = b * BLOCK
    return pl.ds(start if isinstance(start, int) else pl.multiple_of(start, BLOCK), BLOCK)


def down(s, biases):
    return jnp.concatenate(
        [s[b * BLOCK : (b + 1) * BLOCK] * SCALE2 + bias for b, bias in enumerate(biases)], axis=0
    )


def across(s, biases):
    return jnp.concatenate(
        [s[:, b * BLOCK : (b + 1) * BLOCK] * SCALE2 + bias for b, bias in enumerate(biases)], axis=1
    )


def total_of(x):
    return jnp.sum(x, axis=0, keepdims=True)


def pack_kernel(nb, lists, q, k, v, g, out_a, out_b, tiles, sems):
    at = Place(lists, nb)
    copies = []
    for out, partner in zip((out_a, out_b), at.partners):
        for slot, (h, b) in enumerate(partner.sent):
            for i, array in enumerate((q, k, v, g)):
                n = len(copies)
                copy = pltpu.make_async_copy(array.at[rows_of(b), lane(h, 0)], tiles.at[n], sems.at[0, n])
                copy.start()
                copies.append((copy, pltpu.make_async_copy(tiles.at[n], out.at[2 * i + slot], sems.at[1, n])))
    for arrival, departure in copies:
        arrival.wait()
        departure.start()
    for _, departure in copies:
        departure.wait()


def own_forward_kernel(nb, lists, q, k, v, g, stats, ot, out_a, out_b, ps):
    at = Place(lists, nb)
    biases = at.biases()
    for out, partner in zip((out_a, out_b), at.partners):
        for slot, (h, b) in enumerate(partner.sent):
            for i, array in enumerate((q, k, v, g)):
                out[2 * i + slot] = array[rows_of(b), lane(h, 1)]
    for h in range(HEADS):
        cols = lane(h, 0)
        kh, vh = k[:, cols], v[:, cols]
        scores, grads = dot(kh, q[:, cols], 1, 1), dot(vh, g[:, cols], 1, 1)
        for a in range(nb):
            rows = rows_of(a)
            s = down(scores[:, a * BLOCK : (a + 1) * BLOCK], biases[a])
            m = jnp.max(s, axis=0, keepdims=True)
            p = jnp.exp2(s - m)
            stats[h, 0:1, rows] = m
            stats[h, 1:2, rows] = total_of(p)
            stats[h, 2:3, rows] = total_of(p * grads[:, a * BLOCK : (a + 1) * BLOCK])
            ps[:, rows] = p.astype(BF16)
        ot[h] = dot(vh, ps[...], 0, 0)


def split(x):
    parts = []
    for _ in range(3):
        part = x.astype(BF16)
        parts.append(part)
        x = x - part.astype(F32)
    return parts


TILES = 6 * BLOCK


def guest_kernel(nb, half, lists, q, k, v, g, in_a, in_b, stats0, ot0,
                 stats, ot, out_a, out_b, st_a, st_b, aq, pg, dpg):
    at = Place(lists, nb)
    for h in range(2):
        stats[h] = stats0[2 * half + h]
        ot[h] = ot0[2 * half + h]
    aq[...] = jnp.zeros_like(aq)
    kept = []
    for n, (partner, message, out, st) in enumerate(
        zip(at.partners, (in_a, in_b), (out_a, out_b), (st_a, st_b))
    ):
        span = partner.span
        for slot, (h, near, free) in enumerate(partner.guests):
            qg, kg, vg, gg = (message[2 * i + slot] for i in range(4))
            cols = lane(h, half)
            qh, kh, vh, gh = (array[span, cols] for array in (q, k, v, g))
            s = down(dot(kh, qg, 1, 1), near)
            m = jnp.max(s, axis=0, keepdims=True)
            p = jnp.exp2(s - m)
            dp = dot(vh, gg, 1, 1)
            total = total_of(p)
            p = p * (1.0 / total)
            delta = total_of(p * dp)
            st[2 * slot : 2 * slot + 1, :] = m + jnp.log2(total)
            st[2 * slot + 1 : 2 * slot + 2, :] = delta
            weights = p.astype(BF16)
            pg[2 * n + slot] = p
            dpg[2 * n + slot] = dp
            out[rows_of(slot), :] = dot(vh, weights, 0, 0).astype(BF16)
            s = across(dot(kg, qh, 1, 1), free)
            top = jnp.max(s, axis=0, keepdims=True)
            p = jnp.exp2(s - top)
            dp = dot(vg, gh, 1, 1)
            sums = top, total_of(p), total_of(p * dp), dot(vg, p.astype(BF16), 0, 0)
            kept.append((h, partner.span, sums, s, dp, qh, gh, kg))
    for h, span, (top, count, product, out), *_ in kept:
        old = stats[h, 0:1, span]
        m = jnp.maximum(old, top)
        shrink, grow = jnp.exp2(old - m), jnp.exp2(top - m)
        stats[h, 0:1, span] = m
        stats[h, 1:2, span] = stats[h, 1:2, span] * shrink + count * grow
        stats[h, 2:3, span] = stats[h, 2:3, span] * shrink + product * grow
        ot[h, :, span] = ot[h, :, span] * shrink + out * grow
    for h in range(2):
        total = stats[h, 1:2, :]
        stats[h, 3:4, :] = stats[h, 0:1, :] + jnp.log2(total)
        stats[h, 4:5, :] = stats[h, 2:3, :] / total
    for partner, out, st in zip(at.partners, (out_a, out_b), (st_a, st_b)):
        for slot, (h, near, free) in enumerate(partner.guests):
            *_, s, dp, qh, gh, kg = kept.pop(0)
            p = jnp.exp2(s - stats[h, 3:4, partner.span])
            ds = (p * (dp - stats[h, 4:5, partner.span])).astype(BF16)
            out[rows_of(2 + slot), :] = dot(ds, qh, 1, 0).astype(BF16)
            aq[h, partner.span, :] += dot(ds, kg, 0, 0)
            out[rows_of(4 + slot), :] = dot(p.astype(BF16), gh, 1, 0).astype(BF16)
        for slot, (h, b) in enumerate(partner.sent):
            st[4 + 2 * slot : 5 + 2 * slot, :] = stats[h, 3:4, rows_of(b)]
            st[5 + 2 * slot : 6 + 2 * slot, :] = stats[h, 4:5, rows_of(b)]
        for i, part in enumerate(split(st[...])):
            out[TILES + 8 * i : TILES + 8 * i + 8, :] = part


def merged(l1, d1, l2, d2):
    m = jnp.maximum(l1, l2)
    w1, w2 = jnp.exp2(l1 - m), jnp.exp2(l2 - m)
    total = w1 + w2
    return m + jnp.log2(total), (w1 * d1 + w2 * d2) / total


def arrived(came):
    parts = [came[TILES + 8 * i : TILES + 8 * i + 8, :].astype(F32) for i in range(3)]
    return parts[0] + (parts[1] + parts[2])


def whole_guest(slot, mine, got):
    part = mine[2 * slot : 2 * slot + 1, :]
    total, delta = merged(
        part,
        mine[2 * slot + 1 : 2 * slot + 2, :],
        got[4 + 2 * slot : 5 + 2 * slot, :],
        got[5 + 2 * slot : 6 + 2 * slot, :],
    )
    return jnp.exp2(part - total), delta


def return_kernel(nb, half, lists, k, st_a, st_b, pg, dpg, came_a, came_b, *refs):
    back_a, back_b, got_a, got_b = refs[-4:]
    at = Place(lists, nb)
    got_a[...], got_b[...] = arrived(came_a), arrived(came_b)
    for n, (partner, mine, got, back) in enumerate(
        zip(at.partners, (st_a, st_b), (got_a, got_b), (back_a, back_b))
    ):
        if half == 1:
            back[: 2 * BLOCK, :] = refs[n][...]
        for slot, (h, near, free) in enumerate(partner.guests):
            shrink, delta = whole_guest(slot, mine, got)
            ds = (pg[2 * n + slot] * shrink * (dpg[2 * n + slot] - delta)).astype(BF16)
            back[rows_of(2 * half + slot), :] = dot(ds, k[partner.span, lane(h, half)], 0, 0).astype(BF16)


def backward_kernel(
    nb, half, lists, q, k, v, g, in_a, in_b, stats, ot, st_a, st_b, aq0, pg, dpg, came_a, came_b, *refs
):
    outs, kept = refs[-16:-12], refs[-12]
    att, aq, ak, av, fin, ps, dss, got_a, got_b, staged, sems = refs[-11:]
    got_a[...], got_b[...] = arrived(came_a), arrived(came_b)
    at = Place(lists, nb)
    biases = at.biases()
    fin[:, 0:2, :] = stats[:, 3:5, :]
    weights = []
    for partner, got in zip(at.partners, (got_a, got_b)):
        gone = bias_of(partner.there)
        for slot, (h, b) in enumerate(partner.sent):
            rows = rows_of(b)
            part = got[2 * slot : 2 * slot + 1, :] + gone
            total, delta = merged(
                fin[h, 0:1, rows], fin[h, 1:2, rows], part, got[2 * slot + 1 : 2 * slot + 2, :]
            )
            fin[h, 0:1, rows] = total
            fin[h, 1:2, rows] = delta
            weights.append(jnp.exp2(part - total))
    for h in range(2):
        cols = lane(h, half)
        kh = k[:, cols]
        scores, grads = dot(kh, q[:, cols], 1, 1), dot(v[:, cols], g[:, cols], 1, 1)
        own = ot[h] * jnp.exp2(stats[h, 0:1, :] - fin[h, 0:1, :])
        for a in range(nb):
            rows = rows_of(a)
            here = slice(a * BLOCK, (a + 1) * BLOCK)
            att[h, rows, :] = own[:, here].T
            p = jnp.exp2(down(scores[:, here], biases[a]) - fin[h, 0:1, rows])
            ps[:, rows] = p.astype(BF16)
            dss[:, rows] = (p * (grads[:, here] - fin[h, 1:2, rows])).astype(BF16)
        av[h] = dot(ps[...], g[:, cols], 1, 0)
        ak[h] = dot(dss[...], q[:, cols], 1, 0)
        aq[h] = aq0[h] + dot(dss[...], kh, 0, 0)
    for n, (partner, message, mine, got) in enumerate(
        zip(at.partners, (in_a, in_b), (st_a, st_b), (got_a, got_b))
    ):
        for slot, (h, near, free) in enumerate(partner.guests):
            qg, gg = message[slot], message[6 + slot]
            shrink, delta = whole_guest(slot, mine, got)
            p = pg[2 * n + slot] * shrink
            ds = (p * (dpg[2 * n + slot] - delta)).astype(BF16)
            ak[h, partner.span, :] += dot(ds, qg, 1, 0)
            av[h, partner.span, :] += dot(p.astype(BF16), gg, 1, 0)
    for n, (partner, came) in enumerate(zip(at.partners, (came_a, came_b))):
        for slot, (h, b) in enumerate(partner.sent):
            rows = rows_of(b)
            o, dk, dv = (came[rows_of(2 * i + slot), :].astype(F32) for i in range(3))
            att[h, rows, :] += (o * weights[2 * n + slot]).T
            ak[h, rows, :] += dk
            av[h, rows, :] += dv
            kept[2 * n + slot] = aq[h, rows, :]
    copies = []
    for i, (total, scale) in enumerate(((att, 1.0), (aq, SCALE), (ak, SCALE), (av, 1.0))):
        for h in range(2):
            staged[i, :, lane(h, 0)] = (total[h] * scale).astype(BF16)
        there = outs[i].at[:, pl.ds(2 * half * HD, 2 * HD)]
        copies.append(pltpu.make_async_copy(staged.at[i], there, sems.at[i]))
        copies[-1].start()
    for copy in copies:
        copy.wait()


def finish_kernel(nb, lists, before, kept_a, kept_b, last_a, last_b, out, tiles, sems):
    at = Place(lists, nb)
    copies = []
    for n, (partner, last) in enumerate(zip(at.partners, (last_a, last_b))):
        for half, kept in enumerate((kept_a, kept_b)):
            for slot, (h, b) in enumerate(partner.sent):
                value = kept[2 * n + slot] + last[rows_of(2 * half + slot), :].astype(F32)
                i = len(copies)
                tiles[i] = (value * SCALE).astype(BF16)
                copies.append(
                    pltpu.make_async_copy(tiles.at[i], out.at[rows_of(b), lane(h, half)], sems.at[i])
                )
                copies[-1].start()
    for copy in copies:
        copy.wait()


def call(kernel, name, outs, args, scratch=(), flops=0, spaces=None, limit=24 << 20, out=pltpu.VMEM, aliases=None):
    moved = sum(math.prod(s.shape) * s.dtype.itemsize for s in (*outs, *args))
    spaces = spaces or (pltpu.SMEM,) + (pltpu.VMEM,) * (len(args) - 1)
    return pl.pallas_call(
        kernel,
        out_shape=tuple(outs),
        in_specs=[pl.BlockSpec(memory_space=space) for space in spaces],
        out_specs=tuple(pl.BlockSpec(memory_space=o) for o in (out if isinstance(out, tuple) else (out,) * len(outs))),
        scratch_shapes=scratch,
        input_output_aliases=aliases or {},
        cost_estimate=pl.CostEstimate(flops=flops, bytes_accessed=moved if flops else 1, transcendentals=0),
        compiler_params=pltpu.CompilerParams(vmem_limit_bytes=limit),
        name=name,
    )(*args)


def sds(shape, dtype):
    return jax.ShapeDtypeStruct(shape, dtype)


def body(q, k, v, g, lists):
    rows, width = q.shape
    nb = rows // BLOCK
    count = lax.axis_size("seq")

    def pairs(start):
        return [(i, j) for a in range(start, count - 1, 2) for i, j in ((a, a + 1), (a + 1, a))]

    def swap(to_a, to_b):
        return lax.ppermute(to_a, "seq", pairs(0)), lax.ppermute(to_b, "seq", pairs(1))

    arrays = (lists, q, k, v, g)
    tile8 = sds((8, BLOCK, HD), BF16)
    st, acc = sds((8, HD), F32), sds((2, rows, HD), F32)
    first = call(
        functools.partial(pack_kernel, nb), "pack", [tile8] * 2, arrays,
        scratch=(pltpu.VMEM((16, BLOCK, HD), BF16), pltpu.SemaphoreType.DMA((2, 16))),
        spaces=(pltpu.SMEM,) + (pl.ANY,) * 4, limit=60 << 20, out=pl.ANY,
    )
    guests = [swap(*first)]
    stats0, ot0, *second = call(
        functools.partial(own_forward_kernel, nb), "own_forward",
        [sds((HEADS, 8, rows), F32), sds((HEADS, HD, rows), F32), tile8, tile8], arrays, flops=6 << 30,
        scratch=(pltpu.VMEM((rows, rows), BF16),),
    )
    guests.append(swap(*second))
    forward, backs = [], []
    for half in range(2):
        result = sds((TILES + 32, HD), BF16)
        span = (4, 3 * BLOCK, BLOCK)
        *kept, out_a, out_b, st_a, st_b, aq, pg, dpg = call(
            functools.partial(guest_kernel, nb, half), "guest",
            [
                sds((2, 8, rows), F32), sds((2, HD, rows), F32), result, result, st, st,
                acc, sds(span, F32), sds(span, F32),
            ],
            (*arrays, *guests[half], stats0, ot0), flops=4 << 30,
        )
        backs.append(swap(out_a, out_b))
        forward.append((*kept, st_a, st_b, aq, pg, dpg, *backs[half]))
    whole, kepts, returns, outs = sds((rows, width), BF16), [], (), ()
    for half in range(2):
        _, _, st_a, st_b, _, pg, dpg, came_a, came_b = forward[half]
        ours = sds((2 * (1 + half) * BLOCK, HD), BF16)
        returns = call(
            functools.partial(return_kernel, nb, half), "return", [ours, ours],
            (lists, k, st_a, st_b, pg, dpg, came_a, came_b, *returns, *outs[-1:]),
            scratch=(pltpu.VMEM((8, HD), F32), pltpu.VMEM((8, HD), F32)), flops=(40 << 30, 0)[half],
            spaces=(pltpu.SMEM,) + (pltpu.VMEM,) * (7 + len(returns)) + (pl.ANY,) * len(outs[-1:]),
        )
        if half == 1:
            last = swap(*returns)
        before = (returns[0], *outs[:4])
        outs = call(
            functools.partial(backward_kernel, nb, half), "backward",
            [whole] * 4 + [sds((4, BLOCK, HD), F32)], (*arrays, *guests[half], *forward[half], *before),
            scratch=(
                *(pltpu.VMEM((2, rows, HD), F32) for _ in range(4)), pltpu.VMEM((2, 8, rows), F32),
                pltpu.VMEM((rows, rows), BF16), pltpu.VMEM((rows, rows), BF16),
                pltpu.VMEM((8, HD), F32), pltpu.VMEM((8, HD), F32),
                pltpu.VMEM((4, rows, 2 * HD), BF16), pltpu.SemaphoreType.DMA((4,)),
            ), flops=0,
            spaces=(pltpu.SMEM,) + (pltpu.VMEM,) * 15 + (pl.ANY,) * len(before),
            out=(pl.ANY,) * 4 + (pltpu.VMEM,), aliases={17 + i: i for i in range(4)} if half else None,
        )
        kepts.append(outs[4])
    att, dq, dk, dv, _ = outs
    (dq,) = call(
        functools.partial(finish_kernel, nb), "finish", [whole], (lists, dq, *kepts, *last),
        scratch=(pltpu.VMEM((8, BLOCK, HD), BF16), pltpu.SemaphoreType.DMA((8,))),
        spaces=(pltpu.SMEM, pl.ANY) + (pltpu.VMEM,) * 4, out=pl.ANY, aliases={1: 0},
    )
    return att, dq, dk, dv


def solution(mesh):
    spec = P(("dp", "seq"), None)
    return jax.shard_map(
        body, mesh=mesh, in_specs=(spec,) * 5, out_specs=(spec,) * 4, check_vma=False
    )
```

```python
import functools
import math

import jax
import jax.numpy as jnp
from jax import lax
from jax.experimental import pallas as pl
from jax.experimental.pallas import tpu as pltpu
from jax.sharding import PartitionSpec as P

HEADS = 4
HD = 128
BLOCK = 128
KB = 6
SCALE = HD**-0.5
SCALE2 = SCALE * math.log2(math.e)
NEG = -1e30
F32 = jnp.float32
BF16 = jnp.bfloat16


def dot(a, b, ca, cb):
    return lax.dot_general(a, b, (((ca,), (cb,)), ((), ())), preferred_element_type=F32)


def bias_of(cond):
    return jnp.where(cond, 0.0, NEG).astype(F32)


class Place:
    def __init__(self, lists, nb):
        self.nb = nb
        position = lax.axis_index("seq")
        base = position * nb
        self.lo = lo = [lists[a, 0] - base for a in range(nb)]
        self.hi = hi = []
        for a in range(nb):
            top = lists[a, 0]
            for e in range(1, KB):
                top = jnp.maximum(top, lists[a, e])
            hi.append(top - base)
        end = nb - 1
        cut_right = ((lo[end - 1] != lo[end]) | (hi[end - 1] != hi[end])) & (hi[end - 1] >= nb)
        cut_left = ((lo[0] != lo[1]) | (hi[0] != hi[1])) & (lo[1] <= -1)
        r, l = cut_right.astype(jnp.int32), cut_left.astype(jnp.int32)
        odd = lax.rem(position, 2)
        self.partners = []
        for right in (1 - odd, odd):
            is_right = right == 1

            def pick(to_right, to_left):
                return jnp.where(is_right, to_right, to_left)

            partner = Partner()
            partner.there = pick(position < lax.axis_size("seq") - 1, position > 0)
            partner.sent = [(pick(0, 1 - l), pick(end - 1 + r, 0)), (pick(r, 1), pick(end, 1 - l))]
            guests = [(pick(1 - r, 0), pick(nb, -2 + l)), (pick(1, l), pick(nb + 1 - r, -1))]
            first = pick(nb - 3, 0)
            partner.span = pl.ds(pl.multiple_of(first * BLOCK, BLOCK), 3 * BLOCK)
            cut = pick(r, l) == 1
            partner.guests = []
            for h, number in guests:
                near, free = [], []
                for b in range(3):
                    low, high = pick(lo[nb - 3 + b], lo[b]), pick(hi[nb - 3 + b], hi[b])
                    near.append((low <= number) & (number <= high))
                    gone = cut & (is_right if b == 2 else jnp.logical_not(is_right)) if b != 1 else None
                    free.append(near[b] if b == 1 else near[b] & jnp.logical_not(gone))
                partner.guests.append((h, [bias_of(c) for c in near], [bias_of(c) for c in free]))
            self.partners.append(partner)

    def biases(self):
        return [
            [bias_of((self.lo[a] <= b) & (b <= self.hi[a])) for b in range(self.nb)] for a in range(self.nb)
        ]


class Partner:
    pass


def lane(h, half):
    start = (h + 2 * half) * HD
    return pl.ds(start if isinstance(start, int) else pl.multiple_of(start, HD), HD)


def rows_of(b):
    start = b * BLOCK
    return pl.ds(start if isinstance(start, int) else pl.multiple_of(start, BLOCK), BLOCK)


def down(s, biases):
    return jnp.concatenate(
        [s[b * BLOCK : (b + 1) * BLOCK] * SCALE2 + bias for b, bias in enumerate(biases)], axis=0
    )


def across(s, biases):
    return jnp.concatenate(
        [s[:, b * BLOCK : (b + 1) * BLOCK] * SCALE2 + bias for b, bias in enumerate(biases)], axis=1
    )


def total_of(x):
    return jnp.sum(x, axis=0, keepdims=True)


def pack_kernel(nb, lists, q, k, v, g, out_a, out_b, tiles, sems):
    at = Place(lists, nb)
    copies = []
    for out, partner in zip((out_a, out_b), at.partners):
        for slot, (h, b) in enumerate(partner.sent):
            for i, array in enumerate((q, k, v, g)):
                n = len(copies)
                copy = pltpu.make_async_copy(array.at[rows_of(b), lane(h, 0)], tiles.at[n], sems.at[0, n])
                copy.start()
                copies.append((copy, pltpu.make_async_copy(tiles.at[n], out.at[2 * i + slot], sems.at[1, n])))
    for arrival, departure in copies:
        arrival.wait()
        departure.start()
    for _, departure in copies:
        departure.wait()


def own_forward_kernel(nb, lists, q, k, v, g, stats, ot, out_a, out_b, ps):
    at = Place(lists, nb)
    biases = at.biases()
    for out, partner in zip((out_a, out_b), at.partners):
        for slot, (h, b) in enumerate(partner.sent):
            for i, array in enumerate((q, k, v, g)):
                out[2 * i + slot] = array[rows_of(b), lane(h, 1)]
    for h in range(HEADS):
        cols = lane(h, 0)
        kh, vh = k[:, cols], v[:, cols]
        scores, grads = dot(kh, q[:, cols], 1, 1), dot(vh, g[:, cols], 1, 1)
        for a in range(nb):
            rows = rows_of(a)
            s = down(scores[:, a * BLOCK : (a + 1) * BLOCK], biases[a])
            m = jnp.max(s, axis=0, keepdims=True)
            p = jnp.exp2(s - m)
            stats[h, 0:1, rows] = m
            stats[h, 1:2, rows] = total_of(p)
            stats[h, 2:3, rows] = total_of(p * grads[:, a * BLOCK : (a + 1) * BLOCK])
            ps[:, rows] = p.astype(BF16)
        ot[h] = dot(vh, ps[...], 0, 0)


def split(x):
    parts = []
    for _ in range(3):
        part = x.astype(BF16)
        parts.append(part)
        x = x - part.astype(F32)
    return parts


TILES = (6 * BLOCK, 4 * BLOCK)


def guest_kernel(nb, half, lists, q, k, v, g, in_a, in_b, stats0, ot0,
                 stats, ot, out_a, out_b, st_a, st_b, aq, pg, dpg, *late):
    at = Place(lists, nb)
    for h in range(2):
        stats[h] = stats0[2 * half + h]
        ot[h] = ot0[2 * half + h]
    aq[...] = jnp.zeros_like(aq)
    kept = []
    for n, (partner, message, out, st) in enumerate(
        zip(at.partners, (in_a, in_b), (out_a, out_b), (st_a, st_b))
    ):
        span = partner.span
        for slot, (h, near, free) in enumerate(partner.guests):
            qg, kg, vg, gg = (message[2 * i + slot] for i in range(4))
            cols = lane(h, half)
            qh, kh, vh, gh = (array[span, cols] for array in (q, k, v, g))
            s = down(dot(kh, qg, 1, 1), near)
            m = jnp.max(s, axis=0, keepdims=True)
            p = jnp.exp2(s - m)
            dp = dot(vh, gg, 1, 1)
            total = total_of(p)
            p = p * (1.0 / total)
            delta = total_of(p * dp)
            st[2 * slot : 2 * slot + 1, :] = m + jnp.log2(total)
            st[2 * slot + 1 : 2 * slot + 2, :] = delta
            weights = p.astype(BF16)
            pg[2 * n + slot] = p
            dpg[2 * n + slot] = dp
            out[rows_of(slot), :] = dot(vh, weights, 0, 0).astype(BF16)
            s = across(dot(kg, qh, 1, 1), free)
            top = jnp.max(s, axis=0, keepdims=True)
            p = jnp.exp2(s - top)
            dp = dot(vg, gh, 1, 1)
            sums = top, total_of(p), total_of(p * dp), dot(vg, p.astype(BF16), 0, 0)
            kept.append((h, partner.span, sums, s, dp, qh, gh, kg))
    for h, span, (top, count, product, out), *_ in kept:
        old = stats[h, 0:1, span]
        m = jnp.maximum(old, top)
        shrink, grow = jnp.exp2(old - m), jnp.exp2(top - m)
        stats[h, 0:1, span] = m
        stats[h, 1:2, span] = stats[h, 1:2, span] * shrink + count * grow
        stats[h, 2:3, span] = stats[h, 2:3, span] * shrink + product * grow
        ot[h, :, span] = ot[h, :, span] * shrink + out * grow
    for h in range(2):
        total = stats[h, 1:2, :]
        stats[h, 3:4, :] = stats[h, 0:1, :] + jnp.log2(total)
        stats[h, 4:5, :] = stats[h, 2:3, :] / total
    for n, (partner, out, st) in enumerate(zip(at.partners, (out_a, out_b), (st_a, st_b))):
        for slot, (h, near, free) in enumerate(partner.guests):
            *_, s, dp, qh, gh, kg = kept.pop(0)
            p = jnp.exp2(s - stats[h, 3:4, partner.span])
            ds = (p * (dp - stats[h, 4:5, partner.span])).astype(BF16)
            out[rows_of(2 + slot), :] = dot(ds, qh, 1, 0).astype(BF16)
            aq[h, partner.span, :] += dot(ds, kg, 0, 0)
            dv = dot(p.astype(BF16), gh, 1, 0).astype(BF16)
            if half == 0:
                out[rows_of(4 + slot), :] = dv
            else:
                late[n][rows_of(slot), :] = dv
        for slot, (h, b) in enumerate(partner.sent):
            st[4 + 2 * slot : 5 + 2 * slot, :] = stats[h, 3:4, rows_of(b)]
            st[5 + 2 * slot : 6 + 2 * slot, :] = stats[h, 4:5, rows_of(b)]
        for i, part in enumerate(split(st[...])):
            out[TILES[half] + 8 * i : TILES[half] + 8 * i + 8, :] = part


def merged(l1, d1, l2, d2):
    m = jnp.maximum(l1, l2)
    w1, w2 = jnp.exp2(l1 - m), jnp.exp2(l2 - m)
    total = w1 + w2
    return m + jnp.log2(total), (w1 * d1 + w2 * d2) / total


def arrived(half, came):
    first = TILES[half]
    parts = [came[first + 8 * i : first + 8 * i + 8, :].astype(F32) for i in range(3)]
    return parts[0] + (parts[1] + parts[2])


def whole_guest(slot, mine, got):
    part = mine[2 * slot : 2 * slot + 1, :]
    total, delta = merged(
        part,
        mine[2 * slot + 1 : 2 * slot + 2, :],
        got[4 + 2 * slot : 5 + 2 * slot, :],
        got[5 + 2 * slot : 6 + 2 * slot, :],
    )
    return jnp.exp2(part - total), delta


def return_kernel(nb, half, lists, k, st_a, st_b, pg, dpg, came_a, came_b, *refs):
    back_a, back_b, got_a, got_b = refs[-4:]
    at = Place(lists, nb)
    got_a[...], got_b[...] = arrived(half, came_a), arrived(half, came_b)
    for n, (partner, mine, got, back) in enumerate(
        zip(at.partners, (st_a, st_b), (got_a, got_b), (back_a, back_b))
    ):
        if half == 1:
            back[: 2 * BLOCK, :] = refs[n][...]
            back[4 * BLOCK :, :] = refs[2 + n][...]
        for slot, (h, near, free) in enumerate(partner.guests):
            shrink, delta = whole_guest(slot, mine, got)
            ds = (pg[2 * n + slot] * shrink * (dpg[2 * n + slot] - delta)).astype(BF16)
            back[rows_of(2 * half + slot), :] = dot(ds, k[partner.span, lane(h, half)], 0, 0).astype(BF16)


def backward_kernel(
    nb, half, lists, q, k, v, g, in_a, in_b, stats, ot, st_a, st_b, aq0, pg, dpg, came_a, came_b, *refs
):
    outs, kept = refs[-16:-12], refs[-12]
    att, aq, ak, av, fin, ps, dss, got_a, got_b, staged, sems = refs[-11:]
    got_a[...], got_b[...] = arrived(half, came_a), arrived(half, came_b)
    at = Place(lists, nb)
    biases = at.biases()
    fin[:, 0:2, :] = stats[:, 3:5, :]
    weights = []
    for partner, got in zip(at.partners, (got_a, got_b)):
        gone = bias_of(partner.there)
        for slot, (h, b) in enumerate(partner.sent):
            rows = rows_of(b)
            part = got[2 * slot : 2 * slot + 1, :] + gone
            total, delta = merged(
                fin[h, 0:1, rows], fin[h, 1:2, rows], part, got[2 * slot + 1 : 2 * slot + 2, :]
            )
            fin[h, 0:1, rows] = total
            fin[h, 1:2, rows] = delta
            weights.append(jnp.exp2(part - total))
    for h in range(2):
        cols = lane(h, half)
        kh = k[:, cols]
        scores, grads = dot(kh, q[:, cols], 1, 1), dot(v[:, cols], g[:, cols], 1, 1)
        own = ot[h] * jnp.exp2(stats[h, 0:1, :] - fin[h, 0:1, :])
        for a in range(nb):
            rows = rows_of(a)
            here = slice(a * BLOCK, (a + 1) * BLOCK)
            att[h, rows, :] = own[:, here].T
            p = jnp.exp2(down(scores[:, here], biases[a]) - fin[h, 0:1, rows])
            ps[:, rows] = p.astype(BF16)
            dss[:, rows] = (p * (grads[:, here] - fin[h, 1:2, rows])).astype(BF16)
        av[h] = dot(ps[...], g[:, cols], 1, 0)
        ak[h] = dot(dss[...], q[:, cols], 1, 0)
        aq[h] = aq0[h] + dot(dss[...], kh, 0, 0)
    for n, (partner, message, mine, got) in enumerate(
        zip(at.partners, (in_a, in_b), (st_a, st_b), (got_a, got_b))
    ):
        for slot, (h, near, free) in enumerate(partner.guests):
            qg, gg = message[slot], message[6 + slot]
            shrink, delta = whole_guest(slot, mine, got)
            p = pg[2 * n + slot] * shrink
            ds = (p * (dpg[2 * n + slot] - delta)).astype(BF16)
            ak[h, partner.span, :] += dot(ds, qg, 1, 0)
            av[h, partner.span, :] += dot(p.astype(BF16), gg, 1, 0)
    for n, (partner, came) in enumerate(zip(at.partners, (came_a, came_b))):
        for slot, (h, b) in enumerate(partner.sent):
            rows = rows_of(b)
            o, dk = (came[rows_of(2 * i + slot), :].astype(F32) for i in range(2))
            att[h, rows, :] += (o * weights[2 * n + slot]).T
            ak[h, rows, :] += dk
            kept[2 * n + slot] = aq[h, rows, :]
            if half == 0:
                av[h, rows, :] += came[rows_of(4 + slot), :].astype(F32)
            else:
                kept[4 + 2 * n + slot] = av[h, rows, :]
    copies = []
    for i, (total, scale) in enumerate(((att, 1.0), (aq, SCALE), (ak, SCALE), (av, 1.0))):
        for h in range(2):
            staged[i, :, lane(h, 0)] = (total[h] * scale).astype(BF16)
        there = outs[i].at[:, pl.ds(2 * half * HD, 2 * HD)]
        copies.append(pltpu.make_async_copy(staged.at[i], there, sems.at[i]))
        copies[-1].start()
    for copy in copies:
        copy.wait()


def finish_kernel(nb, lists, dq, dv, kept_a, kept_b, last_a, last_b, dq_out, dv_out, tiles, sems):
    at = Place(lists, nb)
    copies = []
    for n, (partner, last) in enumerate(zip(at.partners, (last_a, last_b))):
        for slot, (h, b) in enumerate(partner.sent):
            i = 2 * n + slot
            for half, own, row, scale, out in (
                (0, kept_a[i], slot, SCALE, dq_out),
                (1, kept_b[i], 2 + slot, SCALE, dq_out),
                (1, kept_b[4 + i], 4 + slot, 1.0, dv_out),
            ):
                c = len(copies)
                tiles[c] = ((own + last[rows_of(row), :].astype(F32)) * scale).astype(BF16)
                copies.append(
                    pltpu.make_async_copy(tiles.at[c], out.at[rows_of(b), lane(h, half)], sems.at[c])
                )
                copies[-1].start()
    for copy in copies:
        copy.wait()


def call(kernel, name, outs, args, scratch=(), flops=0, spaces=None, limit=24 << 20, out=pltpu.VMEM, aliases=None):
    moved = sum(math.prod(s.shape) * s.dtype.itemsize for s in (*outs, *args))
    spaces = spaces or (pltpu.SMEM,) + (pltpu.VMEM,) * (len(args) - 1)
    return pl.pallas_call(
        kernel,
        out_shape=tuple(outs),
        in_specs=[pl.BlockSpec(memory_space=space) for space in spaces],
        out_specs=tuple(pl.BlockSpec(memory_space=o) for o in (out if isinstance(out, tuple) else (out,) * len(outs))),
        scratch_shapes=scratch,
        input_output_aliases=aliases or {},
        cost_estimate=pl.CostEstimate(flops=flops, bytes_accessed=moved if flops else 1, transcendentals=0),
        compiler_params=pltpu.CompilerParams(vmem_limit_bytes=limit),
        name=name,
    )(*args)


def sds(shape, dtype):
    return jax.ShapeDtypeStruct(shape, dtype)


def body(q, k, v, g, lists):
    rows, width = q.shape
    nb = rows // BLOCK
    count = lax.axis_size("seq")

    def pairs(start):
        return [(i, j) for a in range(start, count - 1, 2) for i, j in ((a, a + 1), (a + 1, a))]

    def swap(to_a, to_b):
        return lax.ppermute(to_a, "seq", pairs(0)), lax.ppermute(to_b, "seq", pairs(1))

    arrays = (lists, q, k, v, g)
    tile8 = sds((8, BLOCK, HD), BF16)
    st, acc = sds((8, HD), F32), sds((2, rows, HD), F32)
    first = call(
        functools.partial(pack_kernel, nb), "pack", [tile8] * 2, arrays,
        scratch=(pltpu.VMEM((16, BLOCK, HD), BF16), pltpu.SemaphoreType.DMA((2, 16))),
        spaces=(pltpu.SMEM,) + (pl.ANY,) * 4, limit=60 << 20, out=pl.ANY,
    )
    guests = [swap(*first)]
    stats0, ot0, *second = call(
        functools.partial(own_forward_kernel, nb), "own_forward",
        [sds((HEADS, 8, rows), F32), sds((HEADS, HD, rows), F32), tile8, tile8], arrays, flops=6 << 30,
        scratch=(pltpu.VMEM((rows, rows), BF16),),
    )
    guests.append(swap(*second))
    forward, backs = [], []
    for half in range(2):
        result, pair = sds((TILES[half] + 32, HD), BF16), sds((2 * BLOCK, HD), BF16)
        span = (4, 3 * BLOCK, BLOCK)
        fwd, ot, out_a, out_b, st_a, st_b, aq, pg, dpg, *late = call(
            functools.partial(guest_kernel, nb, half), "guest",
            [
                sds((2, 8, rows), F32), sds((2, HD, rows), F32), result, result, st, st,
                acc, sds(span, F32), sds(span, F32), *[pair] * (2 * half),
            ],
            (*arrays, *guests[half], stats0, ot0), flops=4 << 30,
        )
        backs.append(swap(out_a, out_b))
        forward.append((fwd, ot, st_a, st_b, aq, pg, dpg, *backs[half]))
    whole, kepts, returns, outs = sds((rows, width), BF16), [], (), ()
    for half in range(2):
        _, _, st_a, st_b, _, pg, dpg, came_a, came_b = forward[half]
        ours = sds(((2, 6)[half] * BLOCK, HD), BF16)
        returns = (*returns, *late) if half else ()
        returns = call(
            functools.partial(return_kernel, nb, half), "return", [ours, ours],
            (lists, k, st_a, st_b, pg, dpg, came_a, came_b, *returns, *outs[-1:]),
            scratch=(pltpu.VMEM((8, HD), F32), pltpu.VMEM((8, HD), F32)), flops=(40 << 30, 0)[half],
            spaces=(pltpu.SMEM,) + (pltpu.VMEM,) * (7 + len(returns)) + (pl.ANY,) * len(outs[-1:]),
        )
        if half == 1:
            last = swap(*returns)
        before = (returns[0], *outs[:4])
        outs = call(
            functools.partial(backward_kernel, nb, half), "backward",
            [whole] * 4 + [sds((8, BLOCK, HD), F32)], (*arrays, *guests[half], *forward[half], *before),
            scratch=(
                *(pltpu.VMEM((2, rows, HD), F32) for _ in range(4)), pltpu.VMEM((2, 8, rows), F32),
                pltpu.VMEM((rows, rows), BF16), pltpu.VMEM((rows, rows), BF16),
                pltpu.VMEM((8, HD), F32), pltpu.VMEM((8, HD), F32),
                pltpu.VMEM((4, rows, 2 * HD), BF16), pltpu.SemaphoreType.DMA((4,)),
            ), flops=0,
            spaces=(pltpu.SMEM,) + (pltpu.VMEM,) * 15 + (pl.ANY,) * len(before),
            out=(pl.ANY,) * 4 + (pltpu.VMEM,), aliases={17 + i: i for i in range(4)} if half else None,
        )
        kepts.append(outs[4])
    att, dq, dk, dv, _ = outs
    dq, dv = call(
        functools.partial(finish_kernel, nb), "finish", [whole] * 2, (lists, dq, dv, *kepts, *last),
        scratch=(pltpu.VMEM((12, BLOCK, HD), BF16), pltpu.SemaphoreType.DMA((12,))),
        spaces=(pltpu.SMEM, pl.ANY, pl.ANY) + (pltpu.VMEM,) * 4, out=pl.ANY, aliases={1: 0, 2: 1},
    )
    return att, dq, dk, dv


def solution(mesh):
    spec = P(("dp", "seq"), None)
    return jax.shard_map(
        body, mesh=mesh, in_specs=(spec,) * 5, out_specs=(spec,) * 4, check_vma=False
    )
```

```python
import functools
import math

import jax
import jax.numpy as jnp
from jax import lax
from jax.experimental import pallas as pl
from jax.experimental.pallas import tpu as pltpu
from jax.sharding import PartitionSpec as P

HEADS = 4
HD = 128
BLOCK = 128
KB = 6
SCALE = HD**-0.5
SCALE2 = SCALE * math.log2(math.e)
NEG = -1e30
F32 = jnp.float32
BF16 = jnp.bfloat16


def dot(a, b, ca, cb):
    return lax.dot_general(a, b, (((ca,), (cb,)), ((), ())), preferred_element_type=F32)


def bias_of(cond):
    return jnp.where(cond, 0.0, NEG).astype(F32)


class Place:
    def __init__(self, lists, nb):
        self.nb = nb
        position = lax.axis_index("seq")
        base = position * nb
        self.lo = lo = [lists[a, 0] - base for a in range(nb)]
        self.hi = hi = []
        for a in range(nb):
            top = lists[a, 0]
            for e in range(1, KB):
                top = jnp.maximum(top, lists[a, e])
            hi.append(top - base)
        end = nb - 1
        cut_right = ((lo[end - 1] != lo[end]) | (hi[end - 1] != hi[end])) & (hi[end - 1] >= nb)
        cut_left = ((lo[0] != lo[1]) | (hi[0] != hi[1])) & (lo[1] <= -1)
        r, l = cut_right.astype(jnp.int32), cut_left.astype(jnp.int32)
        odd = lax.rem(position, 2)
        self.partners = []
        for right in (1 - odd, odd):
            is_right = right == 1

            def pick(to_right, to_left):
                return jnp.where(is_right, to_right, to_left)

            partner = Partner()
            partner.there = pick(position < lax.axis_size("seq") - 1, position > 0)
            partner.sent = [(pick(0, 1 - l), pick(end - 1 + r, 0)), (pick(r, 1), pick(end, 1 - l))]
            guests = [(pick(1 - r, 0), pick(nb, -2 + l)), (pick(1, l), pick(nb + 1 - r, -1))]
            first = pick(nb - 3, 0)
            partner.span = pl.ds(pl.multiple_of(first * BLOCK, BLOCK), 3 * BLOCK)
            cut = pick(r, l) == 1
            partner.guests = []
            for h, number in guests:
                near, free = [], []
                for b in range(3):
                    low, high = pick(lo[nb - 3 + b], lo[b]), pick(hi[nb - 3 + b], hi[b])
                    near.append((low <= number) & (number <= high))
                    gone = cut & (is_right if b == 2 else jnp.logical_not(is_right)) if b != 1 else None
                    free.append(near[b] if b == 1 else near[b] & jnp.logical_not(gone))
                partner.guests.append((h, [bias_of(c) for c in near], [bias_of(c) for c in free]))
            self.partners.append(partner)

    def biases(self):
        return [
            [bias_of((self.lo[a] <= b) & (b <= self.hi[a])) for b in range(self.nb)] for a in range(self.nb)
        ]


class Partner:
    pass


def lane(h, half):
    start = (h + 2 * half) * HD
    return pl.ds(start if isinstance(start, int) else pl.multiple_of(start, HD), HD)


def rows_of(b):
    start = b * BLOCK
    return pl.ds(start if isinstance(start, int) else pl.multiple_of(start, BLOCK), BLOCK)


def down(s, biases):
    return jnp.concatenate(
        [s[b * BLOCK : (b + 1) * BLOCK] * SCALE2 + bias for b, bias in enumerate(biases)], axis=0
    )


def across(s, biases):
    return jnp.concatenate(
        [s[:, b * BLOCK : (b + 1) * BLOCK] * SCALE2 + bias for b, bias in enumerate(biases)], axis=1
    )


def total_of(x):
    return jnp.sum(x, axis=0, keepdims=True)


def pack_kernel(nb, lists, q, k, v, g, out_a, out_b, tiles, sems):
    at = Place(lists, nb)
    copies = []
    for out, partner in zip((out_a, out_b), at.partners):
        for slot, (h, b) in enumerate(partner.sent):
            for i, array in enumerate((q, k, v, g)):
                n = len(copies)
                copy = pltpu.make_async_copy(array.at[rows_of(b), lane(h, 0)], tiles.at[n], sems.at[0, n])
                copy.start()
                copies.append((copy, pltpu.make_async_copy(tiles.at[n], out.at[2 * i + slot], sems.at[1, n])))
    for arrival, departure in copies:
        arrival.wait()
        departure.start()
    for _, departure in copies:
        departure.wait()


def own_forward_kernel(nb, lists, q, k, v, g, stats, ot, out_a, out_b, ps):
    at = Place(lists, nb)
    biases = at.biases()
    for out, partner in zip((out_a, out_b), at.partners):
        for slot, (h, b) in enumerate(partner.sent):
            for i, array in enumerate((q, k, v, g)):
                out[2 * i + slot] = array[rows_of(b), lane(h, 1)]
    for h in range(HEADS):
        cols = lane(h, 0)
        kh, vh = k[:, cols], v[:, cols]
        scores, grads = dot(kh, q[:, cols], 1, 1), dot(vh, g[:, cols], 1, 1)
        for a in range(nb):
            rows = rows_of(a)
            s = down(scores[:, a * BLOCK : (a + 1) * BLOCK], biases[a])
            m = jnp.max(s, axis=0, keepdims=True)
            p = jnp.exp2(s - m)
            stats[h, 0:1, rows] = m
            stats[h, 1:2, rows] = total_of(p)
            stats[h, 2:3, rows] = total_of(p * grads[:, a * BLOCK : (a + 1) * BLOCK])
            ps[:, rows] = p.astype(BF16)
        ot[h] = dot(vh, ps[...], 0, 0)


def split(x):
    parts = []
    for _ in range(3):
        part = x.astype(BF16)
        parts.append(part)
        x = x - part.astype(F32)
    return parts


TILES = (6 * BLOCK, 4 * BLOCK)


def guest_kernel(nb, half, lists, q, k, v, g, in_a, in_b, stats0, ot0,
                 stats, ot, out_a, out_b, st_a, st_b, aq, pg, dpg, *late):
    at = Place(lists, nb)
    for h in range(2):
        stats[h] = stats0[2 * half + h]
        ot[h] = ot0[2 * half + h]
    aq[...] = jnp.zeros_like(aq)
    kept = []
    for n, (partner, message, out, st) in enumerate(
        zip(at.partners, (in_a, in_b), (out_a, out_b), (st_a, st_b))
    ):
        span = partner.span
        for slot, (h, near, free) in enumerate(partner.guests):
            qg, kg, vg, gg = (message[2 * i + slot] for i in range(4))
            cols = lane(h, half)
            qh, kh, vh, gh = (array[span, cols] for array in (q, k, v, g))
            s = down(dot(kh, qg, 1, 1), near)
            m = jnp.max(s, axis=0, keepdims=True)
            p = jnp.exp2(s - m)
            dp = dot(vh, gg, 1, 1)
            total = total_of(p)
            p = p * (1.0 / total)
            delta = total_of(p * dp)
            st[2 * slot : 2 * slot + 1, :] = m + jnp.log2(total)
            st[2 * slot + 1 : 2 * slot + 2, :] = delta
            weights = p.astype(BF16)
            pg[2 * n + slot] = p
            dpg[2 * n + slot] = dp
            out[rows_of(slot), :] = dot(vh, weights, 0, 0).astype(BF16)
            s = across(dot(kg, qh, 1, 1), free)
            top = jnp.max(s, axis=0, keepdims=True)
            p = jnp.exp2(s - top)
            dp = dot(vg, gh, 1, 1)
            sums = top, total_of(p), total_of(p * dp), dot(vg, p.astype(BF16), 0, 0)
            kept.append((h, partner.span, sums, s, dp, qh, gh, kg))
    for h, span, (top, count, product, out), *_ in kept:
        old = stats[h, 0:1, span]
        m = jnp.maximum(old, top)
        shrink, grow = jnp.exp2(old - m), jnp.exp2(top - m)
        stats[h, 0:1, span] = m
        stats[h, 1:2, span] = stats[h, 1:2, span] * shrink + count * grow
        stats[h, 2:3, span] = stats[h, 2:3, span] * shrink + product * grow
        ot[h, :, span] = ot[h, :, span] * shrink + out * grow
    for h in range(2):
        total = stats[h, 1:2, :]
        stats[h, 3:4, :] = stats[h, 0:1, :] + jnp.log2(total)
        stats[h, 4:5, :] = stats[h, 2:3, :] / total
    for n, (partner, out, st) in enumerate(zip(at.partners, (out_a, out_b), (st_a, st_b))):
        for slot, (h, near, free) in enumerate(partner.guests):
            *_, s, dp, qh, gh, kg = kept.pop(0)
            p = jnp.exp2(s - stats[h, 3:4, partner.span])
            ds = (p * (dp - stats[h, 4:5, partner.span])).astype(BF16)
            out[rows_of(2 + slot), :] = dot(ds, qh, 1, 0).astype(BF16)
            aq[h, partner.span, :] += dot(ds, kg, 0, 0)
            dv = dot(p.astype(BF16), gh, 1, 0).astype(BF16)
            if half == 0:
                out[rows_of(4 + slot), :] = dv
            else:
                late[n][rows_of(slot), :] = dv
        for slot, (h, b) in enumerate(partner.sent):
            st[4 + 2 * slot : 5 + 2 * slot, :] = stats[h, 3:4, rows_of(b)]
            st[5 + 2 * slot : 6 + 2 * slot, :] = stats[h, 4:5, rows_of(b)]
        for i, part in enumerate(split(st[...])):
            out[TILES[half] + 8 * i : TILES[half] + 8 * i + 8, :] = part


def merged(l1, d1, l2, d2):
    m = jnp.maximum(l1, l2)
    w1, w2 = jnp.exp2(l1 - m), jnp.exp2(l2 - m)
    total = w1 + w2
    return m + jnp.log2(total), (w1 * d1 + w2 * d2) / total


def arrived(half, came):
    first = TILES[half]
    parts = [came[first + 8 * i : first + 8 * i + 8, :].astype(F32) for i in range(3)]
    return parts[0] + (parts[1] + parts[2])


def whole_guest(slot, mine, got):
    part = mine[2 * slot : 2 * slot + 1, :]
    total, delta = merged(
        part,
        mine[2 * slot + 1 : 2 * slot + 2, :],
        got[4 + 2 * slot : 5 + 2 * slot, :],
        got[5 + 2 * slot : 6 + 2 * slot, :],
    )
    return jnp.exp2(part - total), delta


def return_kernel(nb, half, lists, k, st_a, st_b, pg, dpg, came_a, came_b, *refs):
    back_a, back_b, got_a, got_b = refs[-4:]
    at = Place(lists, nb)
    got_a[...], got_b[...] = arrived(half, came_a), arrived(half, came_b)
    for n, (partner, mine, got, back) in enumerate(
        zip(at.partners, (st_a, st_b), (got_a, got_b), (back_a, back_b))
    ):
        if half == 1:
            back[: 2 * BLOCK, :] = refs[n][...]
            back[4 * BLOCK :, :] = refs[2 + n][...]
        for slot, (h, near, free) in enumerate(partner.guests):
            shrink, delta = whole_guest(slot, mine, got)
            ds = (pg[2 * n + slot] * shrink * (dpg[2 * n + slot] - delta)).astype(BF16)
            back[rows_of(2 * half + slot), :] = dot(ds, k[partner.span, lane(h, half)], 0, 0).astype(BF16)


def backward_kernel(
    nb, half, lists, q, k, v, g, in_a, in_b, stats, ot, st_a, st_b, aq0, pg, dpg, came_a, came_b, *refs
):
    outs, kept = refs[-16:-12], refs[-12]
    att, aq, ak, av, fin, ps, dss, got_a, got_b, staged, sems = refs[-11:]
    got_a[...], got_b[...] = arrived(half, came_a), arrived(half, came_b)
    at = Place(lists, nb)
    biases = at.biases()
    fin[:, 0:2, :] = stats[:, 3:5, :]
    weights = []
    for partner, got in zip(at.partners, (got_a, got_b)):
        gone = bias_of(partner.there)
        for slot, (h, b) in enumerate(partner.sent):
            rows = rows_of(b)
            part = got[2 * slot : 2 * slot + 1, :] + gone
            total, delta = merged(
                fin[h, 0:1, rows], fin[h, 1:2, rows], part, got[2 * slot + 1 : 2 * slot + 2, :]
            )
            fin[h, 0:1, rows] = total
            fin[h, 1:2, rows] = delta
            weights.append(jnp.exp2(part - total))
    for h in range(2):
        cols = lane(h, half)
        kh = k[:, cols]
        scores, grads = dot(kh, q[:, cols], 1, 1), dot(v[:, cols], g[:, cols], 1, 1)
        own = ot[h] * jnp.exp2(stats[h, 0:1, :] - fin[h, 0:1, :])
        for a in range(nb):
            rows = rows_of(a)
            here = slice(a * BLOCK, (a + 1) * BLOCK)
            att[h, rows, :] = own[:, here].T
            p = jnp.exp2(down(scores[:, here], biases[a]) - fin[h, 0:1, rows])
            ps[:, rows] = p.astype(BF16)
            dss[:, rows] = (p * (grads[:, here] - fin[h, 1:2, rows])).astype(BF16)
        av[h] = dot(ps[...], g[:, cols], 1, 0)
        ak[h] = dot(dss[...], q[:, cols], 1, 0)
        aq[h] = aq0[h] + dot(dss[...], kh, 0, 0)
    copies = []

    def ship(i, total, scale):
        for h in range(2):
            staged[i, :, lane(h, 0)] = (total[h] * scale).astype(BF16)
        there = outs[i].at[:, pl.ds(2 * half * HD, 2 * HD)]
        copies.append(pltpu.make_async_copy(staged.at[i], there, sems.at[i]))
        copies[-1].start()

    for n, (partner, came) in enumerate(zip(at.partners, (came_a, came_b))):
        for slot, (h, b) in enumerate(partner.sent):
            rows = rows_of(b)
            att[h, rows, :] += (came[rows_of(slot), :].astype(F32) * weights[2 * n + slot]).T
            kept[2 * n + slot] = aq[h, rows, :]
    ship(0, att, 1.0)
    ship(1, aq, SCALE)
    for n, (partner, message, mine, got) in enumerate(
        zip(at.partners, (in_a, in_b), (st_a, st_b), (got_a, got_b))
    ):
        for slot, (h, near, free) in enumerate(partner.guests):
            qg, gg = message[slot], message[6 + slot]
            shrink, delta = whole_guest(slot, mine, got)
            p = pg[2 * n + slot] * shrink
            ds = (p * (dpg[2 * n + slot] - delta)).astype(BF16)
            ak[h, partner.span, :] += dot(ds, qg, 1, 0)
            av[h, partner.span, :] += dot(p.astype(BF16), gg, 1, 0)
    for n, (partner, came) in enumerate(zip(at.partners, (came_a, came_b))):
        for slot, (h, b) in enumerate(partner.sent):
            rows = rows_of(b)
            ak[h, rows, :] += came[rows_of(2 + slot), :].astype(F32)
            if half == 0:
                av[h, rows, :] += came[rows_of(4 + slot), :].astype(F32)
            else:
                kept[4 + 2 * n + slot] = av[h, rows, :]
    ship(2, ak, SCALE)
    ship(3, av, 1.0)
    for copy in copies:
        copy.wait()


def finish_kernel(nb, lists, dq, dv, kept_a, kept_b, last_a, last_b, dq_out, dv_out, tiles, sems):
    at = Place(lists, nb)
    copies = []
    for n, (partner, last) in enumerate(zip(at.partners, (last_a, last_b))):
        for slot, (h, b) in enumerate(partner.sent):
            i = 2 * n + slot
            for half, own, row, scale, out in (
                (0, kept_a[i], slot, SCALE, dq_out),
                (1, kept_b[i], 2 + slot, SCALE, dq_out),
                (1, kept_b[4 + i], 4 + slot, 1.0, dv_out),
            ):
                c = len(copies)
                tiles[c] = ((own + last[rows_of(row), :].astype(F32)) * scale).astype(BF16)
                copies.append(
                    pltpu.make_async_copy(tiles.at[c], out.at[rows_of(b), lane(h, half)], sems.at[c])
                )
                copies[-1].start()
    for copy in copies:
        copy.wait()


def call(kernel, name, outs, args, scratch=(), flops=0, spaces=None, limit=24 << 20, out=pltpu.VMEM, aliases=None):
    moved = sum(math.prod(s.shape) * s.dtype.itemsize for s in (*outs, *args))
    spaces = spaces or (pltpu.SMEM,) + (pltpu.VMEM,) * (len(args) - 1)
    return pl.pallas_call(
        kernel,
        out_shape=tuple(outs),
        in_specs=[pl.BlockSpec(memory_space=space) for space in spaces],
        out_specs=tuple(pl.BlockSpec(memory_space=o) for o in (out if isinstance(out, tuple) else (out,) * len(outs))),
        scratch_shapes=scratch,
        input_output_aliases=aliases or {},
        cost_estimate=pl.CostEstimate(flops=flops, bytes_accessed=moved if flops else 1, transcendentals=0),
        compiler_params=pltpu.CompilerParams(vmem_limit_bytes=limit),
        name=name,
    )(*args)


def sds(shape, dtype):
    return jax.ShapeDtypeStruct(shape, dtype)


def body(q, k, v, g, lists):
    rows, width = q.shape
    nb = rows // BLOCK
    count = lax.axis_size("seq")

    def pairs(start):
        return [(i, j) for a in range(start, count - 1, 2) for i, j in ((a, a + 1), (a + 1, a))]

    def swap(to_a, to_b):
        return lax.ppermute(to_a, "seq", pairs(0)), lax.ppermute(to_b, "seq", pairs(1))

    arrays = (lists, q, k, v, g)
    tile8 = sds((8, BLOCK, HD), BF16)
    st, acc = sds((8, HD), F32), sds((2, rows, HD), F32)
    first = call(
        functools.partial(pack_kernel, nb), "pack", [tile8] * 2, arrays,
        scratch=(pltpu.VMEM((16, BLOCK, HD), BF16), pltpu.SemaphoreType.DMA((2, 16))),
        spaces=(pltpu.SMEM,) + (pl.ANY,) * 4, limit=60 << 20, out=pl.ANY,
    )
    guests = [swap(*first)]
    stats0, ot0, *second = call(
        functools.partial(own_forward_kernel, nb), "own_forward",
        [sds((HEADS, 8, rows), F32), sds((HEADS, HD, rows), F32), tile8, tile8], arrays, flops=6 << 30,
        scratch=(pltpu.VMEM((rows, rows), BF16),),
    )
    guests.append(swap(*second))
    forward, backs = [], []
    for half in range(2):
        result, pair = sds((TILES[half] + 32, HD), BF16), sds((2 * BLOCK, HD), BF16)
        span = (4, 3 * BLOCK, BLOCK)
        fwd, ot, out_a, out_b, st_a, st_b, aq, pg, dpg, *late = call(
            functools.partial(guest_kernel, nb, half), "guest",
            [
                sds((2, 8, rows), F32), sds((2, HD, rows), F32), result, result, st, st,
                acc, sds(span, F32), sds(span, F32), *[pair] * (2 * half),
            ],
            (*arrays, *guests[half], stats0, ot0), flops=4 << 30,
        )
        backs.append(swap(out_a, out_b))
        forward.append((fwd, ot, st_a, st_b, aq, pg, dpg, *backs[half]))
    whole, kepts, returns, outs = sds((rows, width), BF16), [], (), ()
    for half in range(2):
        _, _, st_a, st_b, _, pg, dpg, came_a, came_b = forward[half]
        ours = sds(((2, 6)[half] * BLOCK, HD), BF16)
        returns = (*returns, *late) if half else ()
        returns = call(
            functools.partial(return_kernel, nb, half), "return", [ours, ours],
            (lists, k, st_a, st_b, pg, dpg, came_a, came_b, *returns, *outs[-1:]),
            scratch=(pltpu.VMEM((8, HD), F32), pltpu.VMEM((8, HD), F32)), flops=(40 << 30, 0)[half],
            spaces=(pltpu.SMEM,) + (pltpu.VMEM,) * (7 + len(returns)) + (pl.ANY,) * len(outs[-1:]),
        )
        if half == 1:
            last = swap(*returns)
        before = (returns[0], *outs[:4])
        outs = call(
            functools.partial(backward_kernel, nb, half), "backward",
            [whole] * 4 + [sds((8, BLOCK, HD), F32)], (*arrays, *guests[half], *forward[half], *before),
            scratch=(
                *(pltpu.VMEM((2, rows, HD), F32) for _ in range(4)), pltpu.VMEM((2, 8, rows), F32),
                pltpu.VMEM((rows, rows), BF16), pltpu.VMEM((rows, rows), BF16),
                pltpu.VMEM((8, HD), F32), pltpu.VMEM((8, HD), F32),
                pltpu.VMEM((4, rows, 2 * HD), BF16), pltpu.SemaphoreType.DMA((4,)),
            ), flops=0,
            spaces=(pltpu.SMEM,) + (pltpu.VMEM,) * 15 + (pl.ANY,) * len(before),
            out=(pl.ANY,) * 4 + (pltpu.VMEM,), aliases={17 + i: i for i in range(4)} if half else None,
        )
        kepts.append(outs[4])
    att, dq, dk, dv, _ = outs
    dq, dv = call(
        functools.partial(finish_kernel, nb), "finish", [whole] * 2, (lists, dq, dv, *kepts, *last),
        scratch=(pltpu.VMEM((12, BLOCK, HD), BF16), pltpu.SemaphoreType.DMA((12,))),
        spaces=(pltpu.SMEM, pl.ANY, pl.ANY) + (pltpu.VMEM,) * 4, out=pl.ANY, aliases={1: 0, 2: 1},
    )
    return att, dq, dk, dv


def solution(mesh):
    spec = P(("dp", "seq"), None)
    return jax.shard_map(
        body, mesh=mesh, in_specs=(spec,) * 5, out_specs=(spec,) * 4, check_vma=False
    )
```
